256 devices in a mesh: section: 32 (over z, x), tensor: 8 (over y, core).
Axes of the slice: x: 4, y: 4, z: 8, core: 2. Of those that a mesh axis runs over, the one named last changes fastest.
Arguments:
- hidden: bfloat16 [512, 4608], P('section'), may hold values from -16 to 16
- head_weight: bfloat16 [2048, 64, 4608], P('section', 'tensor'), may hold values from -0.3 to 0.3
- panel_section: int32 [2048, 1], replicated, may hold values from 0 to 31; in each aligned block of 64 rows (0 to 63, 64 to 127, ...) at most 2 rows name the same one
- targets: int32 [512], replicated, may hold values from 0 to 131071
Outputs:
- loss: float32 [512], P('section')
- hidden_grad: float32 [512, 4608], P(('section', 'tensor'))
- slot_grads: bfloat16 [32, 32, 2, 64, 4608], P('section', None, None, 'tensor')
The draws below stay inside these ranges and needn't reach their ends.
Inputs may be any that keep to these rules, and one draw needn't show every extreme that they name: `panel_section`: among the 64 panels of one home section, each section is assigned at most 2 of them, and in every draw some home assigns exactly 2 to one section.
All inputs are finite; a program needn't handle non-finite values.
Results may differ from the reference program's by a relative error of at most 0.009.
Values may be sent and summed in bfloat16 or wider, within the bound.
A program may use at most 128 MiB of HBM per device.

```python
import math
import jax
import jax.numpy as jnp
import numpy as np
from jax import lax

D = 4608
PANEL = 64
PAN_DEV = 64
TOK = 512
CAP = 2
NPANEL = 2048
VOCAB = 131072
N_SECTION = 32


def weight_rows(key):
    values = jax.random.normal(key, (NPANEL, PANEL, D), jnp.float32) * (3.0 / math.sqrt(D))
    return jnp.clip(values, -0.296875, 0.296875)


def draw_head_weight(key, part):
    values = weight_rows(key)
    return values.astype(jnp.bfloat16)


def aligned_rows(base, key, values):
    rows = weight_rows(base).reshape(VOCAB, D)
    third, fourth = jax.random.split(jax.random.fold_in(key, 5))
    chosen = jax.random.permutation(third, TOK)[:8]
    pairs = jax.random.randint(fourth, (8, 2), 0, VOCAB)
    first_rows = rows[pairs[:, 0]]
    second_rows = rows[pairs[:, 1]]
    strength = jnp.array([220.0, 220.0, 300.0, 300.0, 440.0, 440.0, 600.0, 600.0], jnp.float32)
    energy = jnp.sum(first_rows * first_rows, axis=1) + jnp.sum(second_rows * second_rows, axis=1)
    aligned = (strength / energy)[:, None] * (first_rows + second_rows)
    return values.at[chosen].set(aligned)


def draw_hidden(key, part):
    base = key
    key = jax.random.fold_in(key, 11)
    first = jax.random.fold_in(key, 0)
    values = jnp.clip(jax.random.normal(first, (TOK, D), jnp.float32), -8.0, 8.0)
    values = aligned_rows(base, key, values)
    return jnp.clip(values, -16.0, 16.0).astype(jnp.bfloat16)


def plant(drawn, rng, low, largest):
    index_at = [jax.random.randint(jax.random.fold_in(rng, axis), (), 0, length) for axis, length in enumerate(drawn.shape)]
    longest = drawn.shape.index(max(drawn.shape))
    neighbour = index_at[:longest] + [(index_at[longest] + 1) % drawn.shape[longest]] + index_at[longest + 1:]
    return drawn.at[tuple(index_at)].set(low).at[tuple(neighbour)].set(largest)


def skewed_wide(stream_key, extent, count, slope):
    weights = [min(1 << octave, count + 1 - (1 << octave)) * (1 << 20) // math.isqrt((1 << octave) ** slope) + 1 for octave in range((count + 1).bit_length()) if 1 << octave <= count]
    deviation = 1 + sum(weights) // (1 << 30)
    grid = np.cumsum(np.array([max(1, weight // deviation) for weight in weights]))
    lot = jax.random.randint(jax.random.fold_in(stream_key, 1), extent, 0, int(grid[len(weights) - 1]))
    start = jnp.left_shift(1, jnp.searchsorted(jnp.asarray(grid, jnp.int32), lot, side="right").astype(jnp.int32))
    grade = start - 1 + jax.random.randint(jax.random.fold_in(stream_key, 4), extent, 0, 1 << 30) % jnp.minimum(start, count + 1 - start)
    return jax.random.permutation(jax.random.fold_in(stream_key, 2), count)[grade].astype(jnp.int32)


def routed_block(key, own, number, rows, number_of, top, limit, slope):
    ranking = jax.random.permutation(key, number_of)
    packed, common = shares(number_of, rows * top, limit, slope, True), shares(number_of, rows * top, limit, slope, False)
    places = jnp.arange(number_of)

    def named(lengths, offset_by):
        used = int((lengths > 0).sum())
        fixed = max(1, used // 4)
        moved = fixed + (places - fixed + offset_by * (used - fixed)) % max(1, number_of - fixed)
        return jnp.zeros((number_of,), jnp.int32).at[ranking[jnp.where(places < fixed, places, moved)]].set(jnp.asarray(lengths, jnp.int32))

    lengths = jnp.where(number % 4 == 0, named(packed, number // 4), named(common, number - number // 4 - 1))
    mixed = jax.random.permutation(jax.random.fold_in(own, 3), number_of)
    donor, taker = mixed[0:number_of // 2 * 2:2], mixed[1:number_of // 2 * 2:2]
    room = jnp.minimum(lengths[donor] - 1, limit - lengths[taker]) // 2
    room = jnp.where((donor == ranking[0]) | (taker == ranking[0]) | (lengths[taker] == 0), 0, jnp.maximum(room, 0))
    moved = jax.random.randint(jax.random.fold_in(own, 4), (number_of // 2,), 0, 1 << 20) % (room + 1)
    lengths = lengths.at[donor].add(-moved).at[taker].add(moved)
    members = jnp.searchsorted(jnp.cumsum(lengths), jnp.arange(rows * top), side="right").astype(jnp.int32)
    grid = members.reshape(top, rows).T
    grid = grid[jax.random.permutation(jax.random.fold_in(own, 1), rows)]
    offset_by = jax.random.randint(jax.random.fold_in(own, 2), (rows, 1), 0, top)
    return jnp.take_along_axis(grid, (jnp.arange(top)[None, :] + offset_by) % top, axis=1)


def shares(number_of, total, reach, skew, full):
    weights = [(1 << 20) // math.isqrt(standing ** skew) + 1 for standing in range(1, number_of + 1)]
    largest = reach if full else min(reach, max(-(-total // number_of), total * weights[0] // sum(weights)))
    least = 1 if total - largest >= number_of - 1 else 0
    given, surplus = [largest] + [least] * (number_of - 1), total - largest - least * (number_of - 1)
    while surplus > 0:
        movable = [i for i in range(1, number_of) if given[i] < largest] or [i for i in range(1, number_of) if given[i] < reach]
        pool, left = sum([weights[i] for i in movable]), surplus
        for i in movable:
            more = min(reach - given[i], max(1, left * weights[i] // pool), surplus)
            given[i] = given[i] + more
            surplus = surplus - more
    return np.array(given)


def setup_inputs(seed: int = 0) -> dict:
    arg_keys = jax.random.split(jax.random.key(seed), 5)
    hidden = draw_hidden(jax.random.fold_in(arg_keys[4], 71), 0)
    head_weight = draw_head_weight(jax.random.fold_in(arg_keys[4], 71), 0)
    panel_section_keys = jax.random.split(jax.random.fold_in(arg_keys[2], 1), NPANEL // PAN_DEV)
    panel_section_turns = jax.random.permutation(jax.random.fold_in(arg_keys[2], 3), NPANEL // PAN_DEV)
    panel_section = jax.vmap(lambda own, number: routed_block(jax.random.fold_in(arg_keys[2], 2), own, number, PAN_DEV, N_SECTION, 1, CAP, 2))(panel_section_keys, panel_section_turns).reshape((NPANEL, 1))
    targets = plant(skewed_wide(arg_keys[3], (TOK,), VOCAB, 2), jax.random.fold_in(arg_keys[3], 3), 0, VOCAB - 1).astype(jnp.int32)
    return dict(hidden=hidden, head_weight=head_weight, panel_section=panel_section, targets=targets)


def home_ranks(dest):
    same = dest[:, :, None] == dest[:, None, :]
    order = jnp.arange(PAN_DEV, dtype=jnp.int32)
    earlier = order[None, :] < order[:, None]
    return jnp.sum((same & earlier[None]).astype(jnp.int32), axis=2).astype(jnp.int32)


def reference(hidden, head_weight, panel_section, targets):
    flat = head_weight.reshape(VOCAB, D)
    logits = lax.dot_general(hidden, flat, (((1,), (1,)), ((), ())), preferred_element_type=jnp.float32)
    top = jnp.max(logits, axis=1)
    shifted = jnp.exp(logits - top[:, None])
    total = jnp.sum(shifted, axis=1)
    picked = jnp.take_along_axis(logits, targets[:, None].astype(jnp.int32), axis=1)[:, 0]
    loss = jnp.log(total) + top - picked
    onehot = (jnp.arange(VOCAB, dtype=jnp.int32)[None, :] == targets[:, None]).astype(jnp.float32)
    dlogits = (shifted / total[:, None] - onehot).astype(jnp.bfloat16)
    hidden_grad = jnp.dot(dlogits, flat, preferred_element_type=jnp.float32)
    dest = panel_section[:, 0].reshape(N_SECTION, PAN_DEV)
    ranks = home_ranks(dest)
    homes = jnp.arange(N_SECTION, dtype=jnp.int32)[:, None] * PAN_DEV + jnp.arange(PAN_DEV, dtype=jnp.int32)[None, :]

    def one_section(target_section):
        match = (dest[:, None, :] == target_section) & (ranks[:, None, :] == jnp.arange(CAP, dtype=jnp.int32)[None, :, None])
        panel_ids = jnp.sum(jnp.where(match, homes[:, None, :], 0), axis=2).astype(jnp.int32)
        live = jnp.any(match, axis=2)
        columns = (panel_ids[:, :, None] * PANEL + jnp.arange(PANEL, dtype=jnp.int32)[None, None, :]).reshape(-1)
        live_cols = jnp.broadcast_to(live[:, :, None], (N_SECTION, CAP, PANEL)).reshape(-1)
        piece = jnp.take(dlogits, columns, axis=1)
        piece = jnp.where(live_cols[None, :], piece, jnp.zeros_like(piece))
        grads = lax.dot_general(piece, hidden, (((0,), (0,)), ((), ())), preferred_element_type=jnp.float32)
        return grads.astype(jnp.bfloat16).reshape(N_SECTION, CAP, PANEL, D)

    slot_grads = lax.map(one_section, jnp.arange(N_SECTION, dtype=jnp.int32))
    return loss, hidden_grad, slot_grads
```

```python
import jax
import jax.numpy as jnp
from jax import lax
from jax.sharding import PartitionSpec as P


def home_ranks(dest):
    count = dest.shape[1]
    same = dest[:, :, None] == dest[:, None, :]
    order = jnp.arange(count, dtype=jnp.int32)
    earlier = order[None, :] < order[:, None]
    return jnp.sum((same & earlier[None]).astype(jnp.int32), axis=2)


def on_device(hidden, head_weight, panel_section, targets):
    sections = lax.axis_size("section")
    tensors = lax.axis_size("tensor")
    myself = lax.axis_index("section")
    portion = lax.axis_index("tensor")
    per_section, rows, width = head_weight.shape
    slots = 5 * per_section // (4 * sections)
    panel_rows = rows * tensors
    dest = panel_section[:, 0].reshape(sections, per_section)
    my_dest = lax.dynamic_index_in_dim(dest, myself, 0, keepdims=True)
    my_rank = home_ranks(my_dest)[0]
    my_dest = my_dest[0]
    section_ids = jnp.arange(sections, dtype=jnp.int32)
    slot_ids = jnp.arange(slots, dtype=jnp.int32)
    send_map = (
        (my_dest[None, None, :] == section_ids[:, None, None])
        & (my_rank[None, None, :] == slot_ids[None, :, None])
    ).reshape(sections * slots, per_section)
    whole = lax.all_gather(hidden, "section", axis=0, tiled=True)
    tokens = whole.shape[0]
    weight = head_weight.reshape(per_section * rows, width)
    logits = lax.dot_general(
        weight, whole, (((1,), (1,)), ((), ())), preferred_element_type=jnp.float32
    )
    row = jnp.arange(per_section * rows, dtype=jnp.int32)
    row_ids = (myself * per_section + row // rows) * panel_rows + portion * rows + row % rows
    hits = row_ids[:, None] == targets[None, :]
    local_top = jnp.max(logits, axis=0)
    local_total = jnp.sum(jnp.exp(logits - local_top[None, :]), axis=0)
    local_picked = jnp.sum(jnp.where(hits, logits, 0.0), axis=0)
    top = lax.pmax(local_top, ("section", "tensor"))
    total, picked = lax.psum(
        (local_total * jnp.exp(local_top - top), local_picked), ("section", "tensor")
    )
    loss = jnp.log(total) + top - picked
    dlogits = (
        jnp.exp(logits - top[None, :]) / total[None, :] - hits.astype(jnp.float32)
    ).astype(jnp.bfloat16)
    packed = jnp.dot(
        send_map.astype(jnp.bfloat16),
        dlogits.reshape(per_section, rows * tokens),
        preferred_element_type=jnp.float32,
    ).astype(jnp.bfloat16)
    arrived = lax.all_to_all(
        packed.reshape(sections, slots * rows, tokens),
        "section",
        split_axis=0,
        concat_axis=0,
        tiled=True,
    )
    partial_grad = lax.dot_general(
        dlogits, weight, (((0,), (0,)), ((), ())), preferred_element_type=jnp.float32
    )
    hidden_grad = lax.psum_scatter(
        partial_grad, ("section", "tensor"), scatter_dimension=0, tiled=True
    )
    grads = lax.dot_general(
        arrived.reshape(sections * slots * rows, tokens),
        whole,
        (((1,), (0,)), ((), ())),
        preferred_element_type=jnp.float32,
    ).astype(jnp.bfloat16)
    slot_grads = grads.reshape(1, sections, slots, rows, width)
    own_rows = hidden.shape[0]
    own_loss = lax.dynamic_slice_in_dim(loss, myself * own_rows, own_rows)
    return (own_loss, hidden_grad, slot_grads)


def solution(mesh):
    in_specs = (P("section", None), P("section", "tensor", None), P(), P())
    out_specs = (
        P("section"),
        P(("section", "tensor"), None),
        P("section", None, None, "tensor", None),
    )
    return jax.shard_map(
        on_device, mesh=mesh, in_specs=in_specs, out_specs=out_specs, check_vma=False
    )
```

```python
import functools

import jax
import jax.numpy as jnp
from jax import lax
from jax.experimental import pallas as pl
from jax.experimental.pallas import tpu as pltpu
from jax.sharding import PartitionSpec as P

MESH = pl.DeviceIdType.MESH
NZ, NX, NY, NC = 8, 4, 4, 2
NS, NT = NZ * NX, NY * NC
D = 4608
TOK = 512
ROWS = 16
VOC = 512
QUART = D // 4
WIDE = 768
NARROW = 384
DX = (1, 3, 2)
NT_DIMS = (((1,), (1,)), ((), ()))


def mod(a, n):
    return lax.rem(a + 2 * n, n)


def body(
    hidden_ref,
    weight_hbm,
    panels_ref,
    targets_ref,
    loss_ref,
    hgrad_ref,
    slots_hbm,
    w,
    hb,
    lbuf,
    dlb,
    pack,
    tcol,
    a2as,
    a2ar,
    st_s,
    st_z,
    st_x,
    st_t,
    r0s,
    r0r,
    own,
    ys,
    yr,
    xs,
    xr,
    x2s,
    x2r,
    acc2,
    y2s,
    y2r,
    zf,
    zs,
    zr,
    fin_s,
    fin_r,
    stage,
    local_sem,
    out_sem,
    gz0,
    gx0,
    gx1,
    gz1,
    gcore,
    bsem,
    asem,
    r0sem,
    ysem,
    xsem,
    x2sem,
    y2sem,
    zsem,
    fsem,
):
    sec = lax.axis_index("section")
    ten = lax.axis_index("tensor")
    z, x = sec // NX, sec % NX
    y, c = ten // NC, ten % NC
    sgn = 1 - 2 * c
    q0, q1 = 2 * c, 2 * c + 1

    def at_z(zz):
        return (zz * NX + x, ten)

    def at_x(xx):
        return (z * NX + xx, ten)

    def at_y(yy):
        return (sec, yy * NC + c)

    other = (sec, y * NC + 1 - c)
    sent = []

    def push(src, dst, sems, where, dev):
        copy = pltpu.make_async_remote_copy(
            src_ref=src,
            dst_ref=dst,
            send_sem=sems.at[(0, *where)],
            recv_sem=sems.at[(1, *where)],
            device_id=dev,
            device_id_type=MESH,
        )
        copy.start()
        sent.append(copy)

    def landed(dst, sems, where):
        pltpu.make_async_copy(dst, dst, sems.at[(1, *where)]).wait()

    w_in = pltpu.make_async_copy(weight_hbm, w, local_sem.at[0])
    w_in.start()
    for part in range(2):
        for core in range(2):
            @pl.when(c == core)
            def _():
                lo = (2 * core + part) * QUART
                hb[2 * core + part, z, x] = hidden_ref[:, lo:lo + QUART]

    barrier = pltpu.get_barrier_semaphore()

    def greet_sections(i, carry):
        pl.semaphore_signal(
            barrier, inc=1, device_id=(mod(sec + i, NS), ten), device_id_type=MESH
        )
        return carry

    lax.fori_loop(1, NS, greet_sections, 0)

    def greet_tensors(i, carry):
        pl.semaphore_signal(
            barrier, inc=1, device_id=(sec, mod(ten + i, NT)), device_id_type=MESH
        )
        return carry

    lax.fori_loop(1, NT, greet_tensors, 0)
    pl.semaphore_wait(barrier, NS - 1 + NT - 1)

    fwd, bwd = at_z(mod(z + sgn, NZ)), at_z(mod(z - sgn, NZ))

    def back(k):
        return mod(z - k * sgn, NZ)

    def ahead(k):
        return mod(z + k * sgn, NZ)

    def send_z(q, sems, zz, xx, way, k, *stream):
        piece = hb.at[q, zz, xx]
        push(piece, piece, sems, (way, k, *stream), fwd if way == 0 else bwd)

    def send_x(q, sems, zz, *where):
        for i, dx in enumerate(DX):
            piece = hb.at[q, zz, x]
            push(piece, piece, sems, (i, *where), at_x(mod(x + dx, NX)))

    streams = [x] + [mod(x - dx, NX) for dx in DX]

    send_z(q0, gz0, z, x, 0, 0)
    send_z(q0, gz0, z, x, 1, 0)
    send_x(q1, gx1, z)
    send_z(q1, gz1, z, x, 0, 0, 0)
    send_z(q1, gz1, z, x, 1, 0, 0)
    send_x(q0, gx0, z, 0)

    w_in.wait()
    lane = lax.broadcasted_iota(jnp.int32, (VOC, VOC), 1)
    row = lax.broadcasted_iota(jnp.int32, (VOC, VOC), 0)
    base = pl.multiple_of((sec // 2) * 128, 128)
    names = panels_ref[:, pl.ds(base, 128)].astype(jnp.float32)
    names = jnp.broadcast_to(names, (8, 128)).astype(jnp.bfloat16)
    spread = (
        lax.broadcasted_iota(jnp.int32, (128, VOC), 0)
        == lax.broadcasted_iota(jnp.int32, (128, VOC), 1) // 8 + (sec % 2) * 64
    )
    named = jnp.dot(
        names, spread.astype(jnp.float32).astype(jnp.bfloat16),
        preferred_element_type=jnp.float32,
    )[:1]
    named_col = jnp.transpose(jnp.broadcast_to(named, (128, VOC)))[:, :1]
    earlier = (named_col == named) & (row // 8 < lane // 8)
    rank = jnp.sum(jnp.where(earlier, 0.125, 0.0), axis=0, keepdims=True)
    wanted = (row // 16).astype(jnp.float32)
    place = (row // 8 % 2).astype(jnp.float32)
    chosen = (wanted == named) & (place == rank) & (row % 8 == lane % 8)
    pack[...] = jnp.where(chosen, 1.0, 0.0).astype(jnp.bfloat16)
    ids = jnp.broadcast_to(targets_ref[...].astype(jnp.float32), (128, TOK))
    tcol[...] = jnp.transpose(ids)

    def step0(k):
        landed(hb.at[q0, back(k + 1), x], gz0, (0, k))
        if k < 3:
            send_z(q0, gz0, back(k + 1), x, 0, k + 1)
        send_x(q0, gx0, back(k + 1), 2 * k + 1)
        if k < 3:
            landed(hb.at[q0, ahead(k + 1), x], gz0, (1, k))
            if k < 2:
                send_z(q0, gz0, ahead(k + 1), x, 1, k + 1)
            send_x(q0, gx0, ahead(k + 1), 2 * k + 2)

    def start1():
        for i in range(3):
            landed(hb.at[q1, z, streams[i + 1]], gx1, (i,))
            send_z(q1, gz1, z, streams[i + 1], 0, 0, i + 1)
            send_z(q1, gz1, z, streams[i + 1], 1, 0, i + 1)
        cross(q1, z, 1, 0)

    def step1(k):
        for i, xx in enumerate(streams):
            landed(hb.at[q1, back(k + 1), xx], gz1, (0, k, i))
            if k < 3:
                send_z(q1, gz1, back(k + 1), xx, 0, k + 1, i)
            if k < 3:
                landed(hb.at[q1, ahead(k + 1), xx], gz1, (1, k, i))
                if k < 2:
                    send_z(q1, gz1, ahead(k + 1), xx, 1, k + 1, i)
        cross(q1, back(k + 1), 1, 2 * k + 1)
        if k < 3:
            cross(q1, ahead(k + 1), 1, 2 * k + 2)

    def cross(q, zz, part, n):
        piece = hb.at[q, zz]
        push(piece, piece, gcore, (part, n), other)

    order = [z]
    for k in range(4):
        order.append(back(k + 1))
        if k < 3:
            order.append(ahead(k + 1))

    def finish0(n):
        for i in range(3):
            landed(hb.at[q0, order[n], streams[i + 1]], gx0, (i, n))
        cross(q0, order[n], 0, n)

    step0(0)
    start1()
    step0(1)
    step1(0)
    step0(2)
    step0(3)
    finish0(0)
    finish0(1)
    finish0(2)
    step1(1)
    finish0(3)
    finish0(4)
    step1(2)
    finish0(5)
    finish0(6)
    step1(3)
    finish0(7)

    def logits(first, last):
        for n in range(first, last):
            mirror = n if n in (0, 7) else (n + 1 if n % 2 else n - 1)
            for part in range(2):
                landed(hb.at[2 - 2 * c + part, order[n]], gcore, (part, mirror))
        count = last - first
        left = jnp.concatenate(
            [
                jnp.concatenate(
                    [hb[q, order[n]].reshape(64, QUART) for n in range(first, last)],
                    axis=0,
                )
                for q in range(4)
            ],
            axis=1,
        )
        product = lax.dot_general(
            left, w[...], NT_DIMS, preferred_element_type=jnp.float32
        )
        for i in range(count):
            lbuf[order[first + i]] = product[i * 64:(i + 1) * 64]

    logits(0, 5)
    logits(5, 8)

    scores = lbuf[...].reshape(TOK, VOC)
    lane1 = lax.broadcasted_iota(jnp.int32, (1, VOC), 1)
    ids_row = (
        (sec * 64 + lane1 // 8) * 64 + ten * 8 + lane1 % 8
    ).astype(jnp.float32)
    hits = tcol[:, :1] == ids_row
    top1 = jnp.max(scores, axis=1, keepdims=True)
    total1 = jnp.sum(jnp.exp(scores - top1), axis=1, keepdims=True)
    picked1 = jnp.sum(jnp.where(hits, scores, 0.0), axis=1, keepdims=True)
    lanes = lax.broadcasted_iota(jnp.int32, (TOK, 128), 1)
    stats = jnp.where(lanes == 0, top1, jnp.where(lanes == 1, total1, picked1))
    st_s[0] = jnp.transpose(stats)[:8]

    def merge(mine, parts):
        tops = [mine[0:1]] + [p[0:1] for p in parts]
        best = functools.reduce(jnp.maximum, tops)
        total = mine[1:2] * jnp.exp(mine[0:1] - best)
        picked = mine[2:3]
        for p in parts:
            total += p[1:2] * jnp.exp(p[0:1] - best)
            picked += p[2:3]
        return best, total, picked

    def rows8(best, total, picked):
        sub = lax.broadcasted_iota(jnp.int32, (8, TOK), 0)
        return jnp.where(sub == 0, best, jnp.where(sub == 1, total, picked))

    for dz in range(1, NZ):
        push(st_s.at[0], st_z.at[dz - 1], bsem, (0, dz - 1), at_z(mod(z + dz, NZ)))
    for dz in range(1, NZ):
        landed(st_z.at[dz - 1], bsem, (0, dz - 1))
    st_s[1] = rows8(*merge(st_s[0], [st_z[i] for i in range(NZ - 1)]))
    for dx in range(1, NX):
        push(st_s.at[1], st_x.at[dx - 1], bsem, (1, dx - 1), at_x(mod(x + dx, NX)))
    for dx in range(1, NX):
        landed(st_x.at[dx - 1], bsem, (1, dx - 1))
    st_s[2] = rows8(*merge(st_s[1], [st_x[i] for i in range(NX - 1)]))
    for dt in range(1, NT):
        push(st_s.at[2], st_t.at[dt - 1], bsem, (2, dt - 1), (sec, mod(ten + dt, NT)))
    for dt in range(1, NT):
        landed(st_t.at[dt - 1], bsem, (2, dt - 1))
    best, total, picked = merge(st_s[2], [st_t[i] for i in range(NT - 1)])
    loss_ref[...] = jnp.log(total) + best - picked
    back_cols = jnp.transpose(
        jnp.concatenate(
            [rows8(best, 1.0 / total, picked), jnp.zeros((120, TOK), jnp.float32)], axis=0
        )
    )
    dl = jnp.exp(scores - back_cols[:, :1]) * back_cols[:, 1:2]
    dlb[...] = (dl - jnp.where(hits, 1.0, 0.0)).astype(jnp.bfloat16)

    half = TOK // 2
    theirs = pl.multiple_of((1 - c) * half, half)
    ours = pl.multiple_of(c * half, half)

    def y_cols(yy):
        return pl.multiple_of(yy * WIDE, WIDE)

    chunks = [
        ("y", mod(y + 2, NY)),
        ("x", 0),
        ("y", mod(y + 1, NY)),
        ("x", 1),
        ("y", mod(y + 3, NY)),
        ("y", y),
    ]
    y_slot = {0: 0, 2: 1, 4: 2}
    x_at = (1, 3)

    def compute(p):
        kind, i = chunks[p]
        lo = y_cols(i) if kind == "y" else NY * WIDE + i * WIDE
        cols = w[:, pl.ds(lo, WIDE)]
        give = jnp.dot(dlb[pl.ds(theirs, half), :], cols, preferred_element_type=jnp.float32)
        r0s[p] = give.astype(jnp.bfloat16).reshape(4, NX, ROWS, WIDE)
        push(r0s.at[p], r0r.at[p], r0sem, (p,), other)
        keep = jnp.dot(dlb[pl.ds(ours, half), :], cols, preferred_element_type=jnp.float32)
        own[p] = keep.reshape(4, NX, ROWS, WIDE)

    def pass_on(p):
        kind, i = chunks[p]
        landed(r0r.at[p], r0sem, (p,))
        both = own[p] + r0r[p].astype(jnp.float32)
        if kind == "x":
            own[p] = both
            xs[i] = both.astype(jnp.bfloat16)
            for n, dx in enumerate(DX):
                push(
                    xs.at[i, :, mod(x + dx, NX)], xr.at[i, n], xsem, (i, n),
                    at_x(mod(x + dx, NX)),
                )
        elif p == 5:
            own[p] = both
        else:
            n = y_slot[p]
            ys[n] = both.astype(jnp.bfloat16)
            push(ys.at[n], yr.at[n], ysem, (n,), at_y(i))

    compute(0)
    compute(1)
    pass_on(0)
    packed = lax.dot_general(
        pack[...], dlb[...], NT_DIMS, preferred_element_type=jnp.float32
    )
    a2as[...] = packed.astype(jnp.bfloat16).reshape(NS, ROWS, TOK)

    def scatter(i, carry):
        to = mod(sec + i, NS)
        pltpu.make_async_remote_copy(
            src_ref=a2as.at[to],
            dst_ref=a2ar.at[sec],
            send_sem=asem.at[0],
            recv_sem=asem.at[1],
            device_id=(to, ten),
            device_id_type=MESH,
        ).start()
        return carry

    lax.fori_loop(1, NS, scatter, 0)
    compute(2)
    pass_on(1)
    compute(3)
    pass_on(2)
    compute(4)
    pass_on(3)
    compute(5)
    pass_on(4)
    pass_on(5)

    for j in range(2):
        for n in range(3):
            landed(xr.at[j, n], xsem, (j, n))
        got = own[x_at[j], :, x]
        for n in range(3):
            got += xr[j, n].astype(jnp.float32)
        for h in range(2):
            piece = got[:, :, h * NARROW:(h + 1) * NARROW]
            acc2[2 * j + h] = piece
            y2s[2 * j + h] = piece.astype(jnp.bfloat16)
    for n in range(3):
        to = mod(y + n + 1, NY)
        push(y2s.at[to], y2r.at[n], y2sem, (n,), at_y(to))

    a2ar[sec] = a2as[sec]
    pltpu.make_async_copy(
        a2ar.at[pl.ds(0, NS - 1)], a2ar.at[pl.ds(0, NS - 1)], asem.at[1]
    ).wait()
    outs = []
    for q in range(4):
        if q >= 2:
            outs[q - 2].wait()
        grads = jnp.dot(
            a2ar[...].reshape(NS * ROWS, TOK),
            hb[q].reshape(TOK, QUART),
            preferred_element_type=jnp.float32,
        )
        stage[q % 2] = grads.astype(jnp.bfloat16)
        out = pltpu.make_async_copy(
            stage.at[q % 2], slots_hbm.at[:, q * QUART:(q + 1) * QUART], out_sem.at[q]
        )
        out.start()
        outs.append(out)

    for n in range(3):
        landed(yr.at[n], ysem, (n,))
    both = own[5]
    for n in range(3):
        both += yr[n].astype(jnp.float32)
    own[5] = both
    x2s[...] = both.astype(jnp.bfloat16)
    for n, dx in enumerate(DX):
        to = mod(x + dx, NX)
        push(x2s.at[:, to], x2r.at[n], x2sem, (n,), at_x(to))

    for n in range(3):
        landed(y2r.at[n], y2sem, (n,))
    narrow = acc2[y]
    for n in range(3):
        narrow += y2r[n].astype(jnp.float32)
    for n in range(3):
        landed(x2r.at[n], x2sem, (n,))
    wide = own[5, :, x]
    for n in range(3):
        wide += x2r[n].astype(jnp.float32)
    zf[:, :, :WIDE] = wide
    zf[:, :, WIDE:] = narrow
    zs[:, :, :WIDE] = wide.astype(jnp.bfloat16)
    zs[:, :, WIDE:] = narrow.astype(jnp.bfloat16)
    mine = z // 4 == c
    z_copies = []
    for i in range(4):
        to = 4 * c + i
        copy = pltpu.make_async_remote_copy(
            src_ref=zs.at[i],
            dst_ref=zr.at[mod(to - z, NZ)],
            send_sem=zsem.at[0, i],
            recv_sem=zsem.at[1, 0],
            device_id=at_z(to),
            device_id_type=MESH,
        )
        z_copies.append((to, copy))

        @pl.when(to != z)
        def _():
            copy.start()

    f_copies = []
    for t in range(NT):
        copy = pltpu.make_async_remote_copy(
            src_ref=fin_s.at[t],
            dst_ref=fin_r.at[y],
            send_sem=fsem.at[0, t],
            recv_sem=fsem.at[1, y],
            device_id=(sec, jnp.int32(t)),
            device_id_type=MESH,
        )
        f_copies.append(copy)

    @pl.when(mine)
    def _():
        zr[0] = jnp.zeros((ROWS, QUART), jnp.bfloat16)
        pltpu.make_async_copy(
            zr.at[pl.ds(1, NZ - 1)], zr.at[pl.ds(1, NZ - 1)], zsem.at[1, 0]
        ).wait()
        final = zf[z % 4]
        for i in range(1, NZ):
            final += zr[i].astype(jnp.float32)
        for t in range(NT):
            fin_s[t] = final[2 * t:2 * t + 2]
        for t in range(NT):
            @pl.when(ten != t)
            def _():
                f_copies[t].start()

        fin_r[y] = fin_s[ten]

    for i in range(NY):
        @pl.when(jnp.logical_not(mine & (y == i)))
        def _():
            landed(fin_r.at[i], fsem, (i,))

        hgrad_ref[:, i * WIDE:(i + 1) * WIDE] = fin_r[i, :, :WIDE]
        hgrad_ref[:, NY * WIDE + i * NARROW:NY * WIDE + (i + 1) * NARROW] = fin_r[
            i, :, WIDE:
        ]

    @pl.when(mine)
    def _():
        for t in range(NT):
            @pl.when(ten != t)
            def _():
                f_copies[t].wait_send()

    for to, copy in z_copies:
        @pl.when(to != z)
        def _():
            copy.wait_send()

    for copy in sent:
        copy.wait_send()
    pltpu.make_async_copy(
        a2as.at[pl.ds(0, NS - 1)], a2as.at[pl.ds(0, NS - 1)], asem.at[0]
    ).wait()
    outs[2].wait()
    outs[3].wait()


def on_device(hidden, head_weight, panel_section, targets):
    per_section, rows, width = head_weight.shape
    bf16, f32 = jnp.bfloat16, jnp.float32
    vmem = pl.BlockSpec(memory_space=pltpu.VMEM)
    hbm = pl.BlockSpec(memory_space=pl.ANY)
    dma = pltpu.SemaphoreType.DMA
    loss, hidden_grad, grads = pl.pallas_call(
        body,
        name="head_step",
        out_shape=(
            jax.ShapeDtypeStruct((1, TOK), f32),
            jax.ShapeDtypeStruct((2, D), f32),
            jax.ShapeDtypeStruct((NS * ROWS, D), bf16),
        ),
        in_specs=[vmem, hbm, vmem, vmem],
        out_specs=(vmem, vmem, hbm),
        scratch_shapes=[
            pltpu.VMEM((VOC, D), bf16),
            pltpu.VMEM((4, NZ, NX, ROWS, QUART), bf16),
            pltpu.VMEM((NZ, 64, VOC), f32),
            pltpu.VMEM((TOK, VOC), bf16),
            pltpu.VMEM((VOC, VOC), bf16),
            pltpu.VMEM((TOK, 128), f32),
            pltpu.VMEM((NS, ROWS, TOK), bf16),
            pltpu.VMEM((NS, ROWS, TOK), bf16),
            pltpu.VMEM((3, 8, TOK), f32),
            pltpu.VMEM((NZ - 1, 8, TOK), f32),
            pltpu.VMEM((NX - 1, 8, TOK), f32),
            pltpu.VMEM((NT - 1, 8, TOK), f32),
            pltpu.VMEM((6, 4, NX, ROWS, WIDE), bf16),
            pltpu.VMEM((6, 4, NX, ROWS, WIDE), bf16),
            pltpu.VMEM((6, 4, NX, ROWS, WIDE), f32),
            pltpu.VMEM((3, 4, NX, ROWS, WIDE), bf16),
            pltpu.VMEM((3, 4, NX, ROWS, WIDE), bf16),
            pltpu.VMEM((2, 4, NX, ROWS, WIDE), bf16),
            pltpu.VMEM((2, 3, 4, ROWS, WIDE), bf16),
            pltpu.VMEM((4, NX, ROWS, WIDE), bf16),
            pltpu.VMEM((3, 4, ROWS, WIDE), bf16),
            pltpu.VMEM((4, 4, ROWS, NARROW), f32),
            pltpu.VMEM((4, 4, ROWS, NARROW), bf16),
            pltpu.VMEM((3, 4, ROWS, NARROW), bf16),
            pltpu.VMEM((4, ROWS, QUART), f32),
            pltpu.VMEM((4, ROWS, QUART), bf16),
            pltpu.VMEM((NZ, ROWS, QUART), bf16),
            pltpu.VMEM((NT, 2, QUART), f32),
            pltpu.VMEM((NY, 2, QUART), f32),
            pltpu.VMEM((2, NS * ROWS, QUART), bf16),
            dma((1,)),
            dma((4,)),
            dma((2, 2, 4)),
            dma((2, 3, 8)),
            dma((2, 3)),
            dma((2, 2, 4, 4)),
            dma((2, 2, 8)),
            dma((2, 3, 7)),
            dma((2,)),
            dma((2, 6)),
            dma((2, 3)),
            dma((2, 2, 3)),
            dma((2, 3)),
            dma((2, 3)),
            dma((2, 4)),
            dma((2, 8)),
        ],
        compiler_params=pltpu.CompilerParams(
            collective_id=0, has_side_effects=True, vmem_limit_bytes=60 * 2**20
        ),
    )(
        hidden,
        head_weight.reshape(per_section * rows, width),
        panel_section.reshape(1, -1),
        targets.reshape(1, -1),
    )
    own_rows = hidden.shape[0]
    myself = lax.axis_index("section")
    own_loss = lax.dynamic_slice_in_dim(loss[0], myself * own_rows, own_rows)
    return (own_loss, hidden_grad, grads.reshape(1, NS, 2, rows, width))


def solution(mesh):
    in_specs = (P("section", None), P("section", "tensor", None), P(), P())
    out_specs = (
        P("section"),
        P(("section", "tensor"), None),
        P("section", None, None, "tensor", None),
    )
    return jax.shard_map(
        on_device, mesh=mesh, in_specs=in_specs, out_specs=out_specs, check_vma=False
    )
```

```python
import functools

import jax
import jax.numpy as jnp
from jax import lax
from jax.experimental import pallas as pl
from jax.experimental.pallas import tpu as pltpu
from jax.sharding import PartitionSpec as P

MESH = pl.DeviceIdType.MESH
NZ, NX, NY, NC = 8, 4, 4, 2
NS, NT = NZ * NX, NY * NC
D = 4608
TOK = 512
ROWS = 16
VOC = 512
QUART = D // 4
WIDE = 768
NARROW = 384
DX = (1, 3, 2)
ROUNDS = (2, 1, 3, 0)
NT_DIMS = (((1,), (1,)), ((), ()))


def mod(a, n):
    return lax.rem(a + 2 * n, n)


def body(
    hidden_ref,
    weight_hbm,
    panels_ref,
    targets_ref,
    loss_ref,
    hgrad_ref,
    slots_ref,
    w,
    hb,
    lbuf,
    dlb,
    pack,
    tcol,
    a2as,
    a2ar,
    st_s,
    st_z,
    st_x,
    st_t,
    r0s,
    r0r,
    own,
    ys,
    yr,
    xs,
    xr,
    x2s,
    x2r,
    acc2,
    y2s,
    y2r,
    zf,
    zsw,
    zsn,
    zrw,
    zrn,
    fin_s,
    fin_r,
    local_sem,
    gz0,
    gx0,
    gx1,
    gz1,
    gcore,
    bsem,
    asem,
    r0sem,
    ysem,
    xsem,
    x2sem,
    y2sem,
    zsem,
    fsem,
):
    sec = lax.axis_index("section")
    ten = lax.axis_index("tensor")
    z, x = sec // NX, sec % NX
    y, c = ten // NC, ten % NC
    sgn = 1 - 2 * c
    q0, q1 = 2 * c, 2 * c + 1

    def at_z(zz):
        return (zz * NX + x, ten)

    def at_x(xx):
        return (z * NX + xx, ten)

    def at_y(yy):
        return (sec, yy * NC + c)

    other = (sec, y * NC + 1 - c)
    sent = []

    def push(src, dst, sems, where, dev):
        copy = pltpu.make_async_remote_copy(
            src_ref=src,
            dst_ref=dst,
            send_sem=sems.at[(0, *where)],
            recv_sem=sems.at[(1, *where)],
            device_id=dev,
            device_id_type=MESH,
        )
        copy.start()
        sent.append(copy)

    def landed(dst, sems, where):
        pltpu.make_async_copy(dst, dst, sems.at[(1, *where)]).wait()

    w_in = pltpu.make_async_copy(weight_hbm, w, local_sem.at[0])
    w_in.start()
    for part in range(2):
        for core in range(2):
            @pl.when(c == core)
            def _():
                lo = (2 * core + part) * QUART
                hb[2 * core + part, z, x] = hidden_ref[:, lo:lo + QUART]

    barrier = pltpu.get_barrier_semaphore()

    def greet_sections(i, carry):
        pl.semaphore_signal(
            barrier, inc=1, device_id=(mod(sec + i, NS), ten), device_id_type=MESH
        )
        return carry

    lax.fori_loop(1, NS, greet_sections, 0)

    def greet_tensors(i, carry):
        pl.semaphore_signal(
            barrier, inc=1, device_id=(sec, mod(ten + i, NT)), device_id_type=MESH
        )
        return carry

    lax.fori_loop(1, NT, greet_tensors, 0)
    pl.semaphore_wait(barrier, NS - 1 + NT - 1)

    fwd, bwd = at_z(mod(z + sgn, NZ)), at_z(mod(z - sgn, NZ))

    def back(k):
        return mod(z - k * sgn, NZ)

    def ahead(k):
        return mod(z + k * sgn, NZ)

    def send_z(q, sems, zz, xx, way, k, *stream):
        piece = hb.at[q, zz, xx]
        push(piece, piece, sems, (way, k, *stream), fwd if way == 0 else bwd)

    def send_x(q, sems, zz, *where):
        for i, dx in enumerate(DX):
            piece = hb.at[q, zz, x]
            push(piece, piece, sems, (i, *where), at_x(mod(x + dx, NX)))

    streams = [x] + [mod(x - dx, NX) for dx in DX]

    send_z(q0, gz0, z, x, 0, 0)
    send_z(q0, gz0, z, x, 1, 0)
    send_x(q1, gx1, z)
    send_z(q1, gz1, z, x, 0, 0, 0)
    send_z(q1, gz1, z, x, 1, 0, 0)
    send_x(q0, gx0, z, 0)

    w_in.wait()
    lane = lax.broadcasted_iota(jnp.int32, (VOC, VOC), 1)
    row = lax.broadcasted_iota(jnp.int32, (VOC, VOC), 0)
    base = pl.multiple_of((sec // 2) * 128, 128)
    names = panels_ref[:, pl.ds(base, 128)].astype(jnp.float32)
    names = jnp.broadcast_to(names, (8, 128)).astype(jnp.bfloat16)
    spread = (
        lax.broadcasted_iota(jnp.int32, (128, VOC), 0)
        == lax.broadcasted_iota(jnp.int32, (128, VOC), 1) // 8 + (sec % 2) * 64
    )
    named = jnp.dot(
        names, spread.astype(jnp.float32).astype(jnp.bfloat16),
        preferred_element_type=jnp.float32,
    )[:1]
    named_col = jnp.transpose(jnp.broadcast_to(named, (128, VOC)))[:, :1]
    earlier = (named_col == named) & (row // 8 < lane // 8)
    rank = jnp.sum(jnp.where(earlier, 0.125, 0.0), axis=0, keepdims=True)
    wanted = (row // 16).astype(jnp.float32)
    place = (row // 8 % 2).astype(jnp.float32)
    chosen = (wanted == named) & (place == rank) & (row % 8 == lane % 8)
    pack[...] = jnp.where(chosen, 1.0, 0.0).astype(jnp.bfloat16)
    ids = jnp.broadcast_to(targets_ref[...].astype(jnp.float32), (128, TOK))
    tcol[...] = jnp.transpose(ids)

    def step0(k):
        landed(hb.at[q0, back(k + 1), x], gz0, (0, k))
        if k < 3:
            send_z(q0, gz0, back(k + 1), x, 0, k + 1)
        send_x(q0, gx0, back(k + 1), 2 * k + 1)
        if k < 3:
            landed(hb.at[q0, ahead(k + 1), x], gz0, (1, k))
            if k < 2:
                send_z(q0, gz0, ahead(k + 1), x, 1, k + 1)
            send_x(q0, gx0, ahead(k + 1), 2 * k + 2)

    def start1():
        for i in range(3):
            landed(hb.at[q1, z, streams[i + 1]], gx1, (i,))
            send_z(q1, gz1, z, streams[i + 1], 0, 0, i + 1)
            send_z(q1, gz1, z, streams[i + 1], 1, 0, i + 1)
        cross(q1, z, 1, 0)

    def step1(k, first, last):
        for i in range(first, last):
            xx = streams[i]
            landed(hb.at[q1, back(k + 1), xx], gz1, (0, k, i))
            if k < 3:
                send_z(q1, gz1, back(k + 1), xx, 0, k + 1, i)
            if k < 3:
                landed(hb.at[q1, ahead(k + 1), xx], gz1, (1, k, i))
                if k < 2:
                    send_z(q1, gz1, ahead(k + 1), xx, 1, k + 1, i)
        if last == 4:
            cross(q1, back(k + 1), 1, 2 * k + 1)
            if k < 3:
                cross(q1, ahead(k + 1), 1, 2 * k + 2)

    def cross(q, zz, part, n):
        piece = hb.at[q, zz]
        push(piece, piece, gcore, (part, n), other)

    order = [z]
    for k in range(4):
        order.append(back(k + 1))
        if k < 3:
            order.append(ahead(k + 1))

    def finish0(n):
        for i in range(3):
            landed(hb.at[q0, order[n], streams[i + 1]], gx0, (i, n))
        cross(q0, order[n], 0, n)

    step0(0)
    start1()
    step1(0, 0, 1)
    step0(1)
    step1(0, 1, 4)
    finish0(0)
    step1(1, 0, 1)
    step0(2)
    step1(1, 1, 4)
    finish0(1)
    finish0(2)
    step1(2, 0, 1)
    step0(3)
    step1(2, 1, 4)
    finish0(3)
    finish0(4)
    step1(3, 0, 4)
    finish0(5)
    finish0(6)
    finish0(7)

    def logits(first, last):
        for n in range(first, last):
            mirror = n if n in (0, 7) else (n + 1 if n % 2 else n - 1)
            for part in range(2):
                landed(hb.at[2 - 2 * c + part, order[n]], gcore, (part, mirror))
        count = last - first
        left = jnp.concatenate(
            [
                jnp.concatenate(
                    [hb[q, order[n]].reshape(64, QUART) for n in range(first, last)],
                    axis=0,
                )
                for q in range(4)
            ],
            axis=1,
        )
        product = lax.dot_general(
            left, w[...], NT_DIMS, preferred_element_type=jnp.float32
        )
        for i in range(count):
            lbuf[order[first + i]] = product[i * 64:(i + 1) * 64]

    logits(0, 5)
    logits(5, 8)

    scores = lbuf[...].reshape(TOK, VOC)
    lane1 = lax.broadcasted_iota(jnp.int32, (1, VOC), 1)
    ids_row = (
        (sec * 64 + lane1 // 8) * 64 + ten * 8 + lane1 % 8
    ).astype(jnp.float32)
    hits = tcol[:, :1] == ids_row
    top1 = jnp.max(scores, axis=1, keepdims=True)
    total1 = jnp.sum(jnp.exp(scores - top1), axis=1, keepdims=True)
    picked1 = jnp.sum(jnp.where(hits, scores, 0.0), axis=1, keepdims=True)
    lanes = lax.broadcasted_iota(jnp.int32, (TOK, 128), 1)
    stats = jnp.where(lanes == 0, top1, jnp.where(lanes == 1, total1, picked1))
    stats = jnp.transpose(stats)
    mine3 = (stats[0:1], stats[1:2], stats[2:3])

    def triple(ref, i):
        return tuple(ref[i, :, n * TOK:(n + 1) * TOK] for n in range(3))

    def merge(mine, parts):
        best = functools.reduce(jnp.maximum, [p[0] for p in parts], mine[0])
        total = mine[1] * jnp.exp(mine[0] - best)
        picked = mine[2]
        for p in parts:
            total += p[1] * jnp.exp(p[0] - best)
            picked += p[2]
        return best, total, picked

    def share(mine, phase, got, count, device):
        for n in range(3):
            st_s[phase, :, n * TOK:(n + 1) * TOK] = mine[n]
        for i in range(1, count):
            push(st_s.at[phase], got.at[i - 1], bsem, (phase, i - 1), device(i))
        for i in range(1, count):
            landed(got.at[i - 1], bsem, (phase, i - 1))
        return merge(mine, [triple(got, i) for i in range(count - 1)])

    def rows8(best, total, picked):
        sub = lax.broadcasted_iota(jnp.int32, (8, TOK), 0)
        return jnp.where(sub == 0, best, jnp.where(sub == 1, total, picked))

    mine3 = share(mine3, 0, st_z, NZ, lambda i: at_z(mod(z + i, NZ)))
    mine3 = share(mine3, 1, st_x, NX, lambda i: at_x(mod(x + i, NX)))
    best, total, picked = share(
        mine3, 2, st_t, NT, lambda i: (sec, mod(ten + i, NT))
    )
    loss = jnp.broadcast_to(jnp.log(total) + best - picked, (8, TOK))
    loss_ref[...] = pltpu.roll(loss, TOK - sec * ROWS, 1)[:1, :ROWS]
    back_cols = jnp.transpose(
        jnp.concatenate(
            [rows8(best, 1.0 / total, picked), jnp.zeros((120, TOK), jnp.float32)], axis=0
        )
    )
    dl = jnp.exp(scores - back_cols[:, :1]) * back_cols[:, 1:2]
    dlb[...] = (dl - jnp.where(hits, 1.0, 0.0)).astype(jnp.bfloat16)

    half = TOK // 2
    theirs = pl.multiple_of((1 - c) * half, half)
    ours = pl.multiple_of(c * half, half)

    def y_cols(yy):
        return pl.multiple_of(yy * WIDE, WIDE)

    chunks = [
        ("y", mod(y + 2, NY)),
        ("x", 0),
        ("y", mod(y + 1, NY)),
        ("x", 1),
        ("y", mod(y + 3, NY)),
        ("y", y),
    ]
    y_slot = {0: 0, 2: 1, 4: 2}
    x_at = (1, 3)

    def compute(p):
        kind, i = chunks[p]
        lo = y_cols(i) if kind == "y" else NY * WIDE + i * WIDE
        cols = w[:, pl.ds(lo, WIDE)]
        give = jnp.dot(dlb[pl.ds(theirs, half), :], cols, preferred_element_type=jnp.float32)
        r0s[p] = give.astype(jnp.bfloat16).reshape(4, NX, ROWS, WIDE)
        push(r0s.at[p], r0r.at[p], r0sem, (p,), other)
        keep = jnp.dot(dlb[pl.ds(ours, half), :], cols, preferred_element_type=jnp.float32)
        own[p] = keep.reshape(4, NX, ROWS, WIDE)

    def send_y(p, r):
        n, to = y_slot[p], mod(x + ROUNDS[r], NX)
        push(ys.at[n, :, to], yr.at[n, :, to], ysem, (n, r), at_y(chunks[p][1]))

    def pass_on(p):
        kind, i = chunks[p]
        landed(r0r.at[p], r0sem, (p,))
        both = own[p] + r0r[p].astype(jnp.float32)
        if kind == "x":
            own[p] = both
            xs[i] = both.astype(jnp.bfloat16)
            for n, dx in enumerate(DX):
                push(
                    xs.at[i, :, mod(x + dx, NX)], xr.at[i, n], xsem, (i, n),
                    at_x(mod(x + dx, NX)),
                )
        elif p == 5:
            own[p] = both
        else:
            n = y_slot[p]
            ys[n] = both.astype(jnp.bfloat16)
            send_y(p, 0)

    compute(0)
    compute(1)
    pass_on(0)
    packed = lax.dot_general(
        pack[...], dlb[...], NT_DIMS, preferred_element_type=jnp.float32
    )
    a2as[...] = packed.astype(jnp.bfloat16).reshape(NS, ROWS, TOK)

    def scatter(i, carry):
        to = mod(sec + i, NS)
        pltpu.make_async_remote_copy(
            src_ref=a2as.at[to],
            dst_ref=a2ar.at[sec],
            send_sem=asem.at[0],
            recv_sem=asem.at[1],
            device_id=(to, ten),
            device_id_type=MESH,
        ).start()
        return carry

    lax.fori_loop(1, NS, scatter, 0)
    compute(2)
    pass_on(1)
    compute(3)
    pass_on(2)
    compute(4)
    pass_on(3)
    compute(5)
    pass_on(4)
    pass_on(5)

    for r in range(1, 4):
        for p in (0, 2, 4):
            send_y(p, r)

    def gather_y(r):
        to = mod(x + ROUNDS[r], NX)
        for n in range(3):
            landed(yr.at[n, :, to], ysem, (n, r))
        both = own[5, :, to]
        for n in range(3):
            both += yr[n, :, to].astype(jnp.float32)
        if r < 3:
            x2s[:, to] = both.astype(jnp.bfloat16)
            push(x2s.at[:, to], x2r.at[r], x2sem, (r,), at_x(to))
        return both

    def gather_x():
        for j in range(2):
            for n in range(3):
                landed(xr.at[j, n], xsem, (j, n))
            got = own[x_at[j], :, x]
            for n in range(3):
                got += xr[j, n].astype(jnp.float32)
            for h in range(2):
                piece = got[:, :, h * NARROW:(h + 1) * NARROW]
                acc2[2 * j + h] = piece
                y2s[2 * j + h] = piece.astype(jnp.bfloat16)
        for n in range(3):
            to = mod(y + n + 1, NY)
            push(y2s.at[to], y2r.at[n], y2sem, (n,), at_y(to))

    def weight_grads(q):
        grads = jnp.dot(
            a2ar[...].reshape(NS * ROWS, TOK),
            hb[q].reshape(TOK, QUART),
            preferred_element_type=jnp.float32,
        )
        slots_ref[:, q * QUART:(q + 1) * QUART] = grads.astype(jnp.bfloat16)

    z_copies = []

    def send_sections(part, src, dst):
        for i in range(4):
            to = 4 * c + i
            copy = pltpu.make_async_remote_copy(
                src_ref=src.at[i],
                dst_ref=dst.at[mod(to - z, NZ)],
                send_sem=zsem.at[0, part, i],
                recv_sem=zsem.at[1, part, 0],
                device_id=at_z(to),
                device_id_type=MESH,
            )
            z_copies.append((to, copy))

            @pl.when(to != z)
            def _():
                copy.start()

    gather_y(0)
    gather_y(1)
    gather_x()
    gather_y(2)
    a2ar[sec] = a2as[sec]
    pltpu.make_async_copy(
        a2ar.at[pl.ds(0, NS - 1)], a2ar.at[pl.ds(0, NS - 1)], asem.at[1]
    ).wait()
    weight_grads(0)
    weight_grads(1)
    wide = gather_y(3)
    for n in range(3):
        landed(x2r.at[n], x2sem, (n,))
        wide += x2r[n].astype(jnp.float32)
    zf[:, :, :WIDE] = wide
    zsw[...] = wide.astype(jnp.bfloat16)
    send_sections(0, zsw, zrw)
    narrow = acc2[y]
    for n in range(3):
        landed(y2r.at[n], y2sem, (n,))
        narrow += y2r[n].astype(jnp.float32)
    zf[:, :, WIDE:] = narrow
    zsn[...] = narrow.astype(jnp.bfloat16)
    send_sections(1, zsn, zrn)
    weight_grads(2)
    weight_grads(3)
    mine = z // 4 == c

    f_copies = []
    for t in range(NT):
        copy = pltpu.make_async_remote_copy(
            src_ref=fin_s.at[t],
            dst_ref=fin_r.at[y],
            send_sem=fsem.at[0, t],
            recv_sem=fsem.at[1, y],
            device_id=(sec, jnp.int32(t)),
            device_id_type=MESH,
        )
        f_copies.append(copy)

    @pl.when(mine)
    def _():
        for part, got in enumerate((zrw, zrn)):
            pltpu.make_async_copy(
                got.at[pl.ds(1, NZ - 1)], got.at[pl.ds(1, NZ - 1)], zsem.at[1, part, 0]
            ).wait()
        high, low = zf[z % 4, :, :WIDE], zf[z % 4, :, WIDE:]
        for i in range(1, NZ):
            high += zrw[i].astype(jnp.float32)
            low += zrn[i].astype(jnp.float32)
        final = jnp.concatenate([high, low], axis=1)
        for t in range(NT):
            fin_s[t] = final[2 * t:2 * t + 2]
        for t in range(NT):
            @pl.when(ten != t)
            def _():
                f_copies[t].start()

        fin_r[y] = fin_s[ten]

    for i in range(NY):
        @pl.when(jnp.logical_not(mine & (y == i)))
        def _():
            landed(fin_r.at[i], fsem, (i,))

        hgrad_ref[:, i * WIDE:(i + 1) * WIDE] = fin_r[i, :, :WIDE]
        hgrad_ref[:, NY * WIDE + i * NARROW:NY * WIDE + (i + 1) * NARROW] = fin_r[
            i, :, WIDE:
        ]

    @pl.when(mine)
    def _():
        for t in range(NT):
            @pl.when(ten != t)
            def _():
                f_copies[t].wait_send()

    for to, copy in z_copies:
        @pl.when(to != z)
        def _():
            copy.wait_send()

    for copy in sent:
        copy.wait_send()
    pltpu.make_async_copy(
        a2as.at[pl.ds(0, NS - 1)], a2as.at[pl.ds(0, NS - 1)], asem.at[0]
    ).wait()


def on_device(hidden, head_weight, panel_section, targets):
    per_section, rows, width = head_weight.shape
    bf16, f32 = jnp.bfloat16, jnp.float32
    vmem = pl.BlockSpec(memory_space=pltpu.VMEM)
    hbm = pl.BlockSpec(memory_space=pl.ANY)
    dma = pltpu.SemaphoreType.DMA
    loss, hidden_grad, grads = pl.pallas_call(
        body,
        name="head_step",
        out_shape=(
            pltpu.VMEM((1, ROWS), f32),
            pltpu.VMEM((2, D), f32),
            pltpu.VMEM((NS * ROWS, D), bf16),
        ),
        in_specs=[vmem, hbm, vmem, vmem],
        out_specs=(vmem, vmem, vmem),
        scratch_shapes=[
            pltpu.VMEM((VOC, D), bf16),
            pltpu.VMEM((4, NZ, NX, ROWS, QUART), bf16),
            pltpu.VMEM((NZ, 64, VOC), f32),
            pltpu.VMEM((TOK, VOC), bf16),
            pltpu.VMEM((VOC, VOC), bf16),
            pltpu.VMEM((TOK, 128), f32),
            pltpu.VMEM((NS, ROWS, TOK), bf16),
            pltpu.VMEM((NS, ROWS, TOK), bf16),
            pltpu.VMEM((3, 1, 3 * TOK), f32),
            pltpu.VMEM((NZ - 1, 1, 3 * TOK), f32),
            pltpu.VMEM((NX - 1, 1, 3 * TOK), f32),
            pltpu.VMEM((NT - 1, 1, 3 * TOK), f32),
            pltpu.VMEM((6, 4, NX, ROWS, WIDE), bf16),
            pltpu.VMEM((6, 4, NX, ROWS, WIDE), bf16),
            pltpu.VMEM((6, 4, NX, ROWS, WIDE), f32),
            pltpu.VMEM((3, 4, NX, ROWS, WIDE), bf16),
            pltpu.VMEM((3, 4, NX, ROWS, WIDE), bf16),
            pltpu.VMEM((2, 4, NX, ROWS, WIDE), bf16),
            pltpu.VMEM((2, 3, 4, ROWS, WIDE), bf16),
            pltpu.VMEM((4, NX, ROWS, WIDE), bf16),
            pltpu.VMEM((3, 4, ROWS, WIDE), bf16),
            pltpu.VMEM((4, 4, ROWS, NARROW), f32),
            pltpu.VMEM((4, 4, ROWS, NARROW), bf16),
            pltpu.VMEM((3, 4, ROWS, NARROW), bf16),
            pltpu.VMEM((4, ROWS, QUART), f32),
            pltpu.VMEM((4, ROWS, WIDE), bf16),
            pltpu.VMEM((4, ROWS, NARROW), bf16),
            pltpu.VMEM((NZ, ROWS, WIDE), bf16),
            pltpu.VMEM((NZ, ROWS, NARROW), bf16),
            pltpu.VMEM((NT, 2, QUART), f32),
            pltpu.VMEM((NY, 2, QUART), f32),
            dma((1,)),
            dma((2, 2, 4)),
            dma((2, 3, 8)),
            dma((2, 3)),
            dma((2, 2, 4, 4)),
            dma((2, 2, 8)),
            dma((2, 3, 7)),
            dma((2,)),
            dma((2, 6)),
            dma((2, 3, 4)),
            dma((2, 2, 3)),
            dma((2, 3)),
            dma((2, 3)),
            dma((2, 2, 4)),
            dma((2, 8)),
        ],
        compiler_params=pltpu.CompilerParams(
            collective_id=0, has_side_effects=True, vmem_limit_bytes=48 * 2**20
        ),
    )(
        hidden,
        head_weight.reshape(per_section * rows, width),
        panel_section.reshape(1, -1),
        targets.reshape(1, -1),
    )
    return (loss.reshape(ROWS), hidden_grad, grads.reshape(1, NS, 2, rows, width))


def solution(mesh):
    in_specs = (P("section", None), P("section", "tensor", None), P(), P())
    out_specs = (
        P("section"),
        P(("section", "tensor"), None),
        P("section", None, None, "tensor", None),
    )
    return jax.shard_map(
        on_device, mesh=mesh, in_specs=in_specs, out_specs=out_specs, check_vma=False
    )
```

```python
import functools

import jax
import jax.numpy as jnp
from jax import lax
from jax.experimental import pallas as pl
from jax.experimental.pallas import tpu as pltpu
from jax.sharding import PartitionSpec as P

MESH = pl.DeviceIdType.MESH
NZ, NX, NY, NC = 8, 4, 4, 2
NS, NT = NZ * NX, NY * NC
D = 4608
TOK = 512
ROWS = 16
VOC = 512
QUART = D // 4
WIDE = 896
CROSS = 512
NARROW = 256
DX = (1, 3, 2)
ROUNDS = (2, 1, 3, 0)
NT_DIMS = (((1,), (1,)), ((), ()))


def mod(a, n):
    return lax.rem(a + 2 * n, n)


def body(
    hidden_hbm,
    weight_hbm,
    panels_hbm,
    targets_hbm,
    loss_ref,
    hgrad_ref,
    slots_ref,
    panels_ref,
    targets_ref,
    w,
    hb,
    lbuf,
    dlb,
    pack,
    tcol,
    a2as,
    a2ar,
    st_s,
    st_z,
    st_x,
    st_t,
    r0s,
    r0r,
    own,
    r0sx,
    r0rx,
    ownx,
    tr,
    ys,
    yr,
    xs,
    xr,
    x2s,
    x2r,
    acc2,
    y2s,
    y2r,
    zf,
    zsw,
    zsn,
    zrw,
    zrn,
    fin_s,
    fin_r,
    local_sem,
    gz,
    gx0,
    gx1,
    gy1,
    gcore,
    bsem,
    asem,
    r0sem,
    trsem,
    ysem,
    xsem,
    x2sem,
    y2sem,
    zsem,
    fsem,
):
    sec = lax.axis_index("section")
    ten = lax.axis_index("tensor")
    z, x = sec // NX, sec % NX
    y, c = ten // NC, ten % NC
    sgn = 1 - 2 * c
    q0, q1 = 2 * c, 2 * c + 1

    def at_z(zz):
        return (zz * NX + x, ten)

    def at_x(xx):
        return (z * NX + xx, ten)

    def at_y(yy):
        return (sec, yy * NC + c)

    other = (sec, y * NC + 1 - c)
    sent = []

    def push(src, dst, sems, where, dev):
        copy = pltpu.make_async_remote_copy(
            src_ref=src,
            dst_ref=dst,
            send_sem=sems.at[(0, *where)],
            recv_sem=sems.at[(1, *where)],
            device_id=dev,
            device_id_type=MESH,
        )
        copy.start()
        sent.append(copy)

    def landed(dst, sems, where):
        pltpu.make_async_copy(dst, dst, sems.at[(1, *where)]).wait()

    own_in = []
    for part in range(2):
        for core in range(2):
            lo = (2 * core + part) * QUART
            copy = pltpu.make_async_copy(
                hidden_hbm.at[:, lo:lo + QUART],
                hb.at[2 * core + part, z, x],
                local_sem.at[1 + part],
            )
            own_in.append((core, copy))

            @pl.when(c == core)
            def _():
                copy.start()

    names_in = pltpu.make_async_copy(panels_hbm, panels_ref, local_sem.at[3])
    names_in.start()
    targets_in = pltpu.make_async_copy(targets_hbm, targets_ref, local_sem.at[4])
    targets_in.start()
    w_in = pltpu.make_async_copy(weight_hbm, w, local_sem.at[0])
    w_in.start()
    barrier = pltpu.get_barrier_semaphore()

    def greet_sections(i, carry):
        pl.semaphore_signal(
            barrier, inc=1, device_id=(mod(sec + i, NS), ten), device_id_type=MESH
        )
        return carry

    lax.fori_loop(1, NS, greet_sections, 0)

    def greet_tensors(i, carry):
        pl.semaphore_signal(
            barrier, inc=1, device_id=(sec, mod(ten + i, NT)), device_id_type=MESH
        )
        return carry

    lax.fori_loop(1, NT, greet_tensors, 0)
    for core, copy in own_in:
        @pl.when(c == core)
        def _():
            copy.wait()

    pl.semaphore_wait(barrier, NS - 1 + NT - 1)

    def back(k):
        return mod(z - k * sgn, NZ)

    def ahead(k):
        return mod(z + k * sgn, NZ)

    order = [z] + [back((n + 1) // 2) if n % 2 else ahead(n // 2) for n in range(1, 8)]
    streams = [x] + [mod(x - dx, NX) for dx in DX]
    mine_x = mod(x + y, NX)

    def send_z(part, q, n, xx, to, arrives):
        piece = hb.at[q, order[n], xx]
        push(piece, piece, gz, (part, arrives), at_z(order[to]))

    def spread_z(part, q, xx):
        for to, arrives in ((2, 1), (1, 2), (4, 3), (3, 4)):
            send_z(part, q, 0, xx, to, arrives)

    def relay_z(part, q, n, xx):
        landed(hb.at[q, order[n], xx], gz, (part, n))
        if n == 3:
            send_z(part, q, 3, xx, 2, 5)
            send_z(part, q, 3, xx, 4, 7)
        if n == 4:
            send_z(part, q, 4, xx, 1, 6)

    def send_x0(n):
        piece = hb.at[q0, order[n], x]
        for i, dx in enumerate(DX):
            push(piece, piece, gx0, (i, n), at_x(mod(x + dx, NX)))

    def send_y1(n):
        piece = hb.at[q1, order[n], mine_x]
        for i in range(3):
            push(piece, piece, gy1, (i, n), at_y(mod(y + 1 + i, NY)))

    def cross(q, part, n):
        piece = hb.at[q, order[n]]
        push(piece, piece, gcore, (part, n), other)

    for i, dx in enumerate(DX):
        push(hb.at[q1, z, x], hb.at[q1, z, x], gx1, (i,), at_x(mod(x + dx, NX)))
    spread_z(0, q0, x)
    send_x0(0)

    names_in.wait()
    targets_in.wait()
    lane = lax.broadcasted_iota(jnp.int32, (VOC, VOC), 1)
    row = lax.broadcasted_iota(jnp.int32, (VOC, VOC), 0)
    base = pl.multiple_of((sec // 2) * 128, 128)
    names = panels_ref[:, pl.ds(base, 128)].astype(jnp.float32)
    names = jnp.broadcast_to(names, (8, 128)).astype(jnp.bfloat16)
    spread = (
        lax.broadcasted_iota(jnp.int32, (128, VOC), 0)
        == lax.broadcasted_iota(jnp.int32, (128, VOC), 1) // 8 + (sec % 2) * 64
    )
    named = jnp.dot(
        names, spread.astype(jnp.float32).astype(jnp.bfloat16),
        preferred_element_type=jnp.float32,
    )[:1]
    named_col = jnp.transpose(jnp.broadcast_to(named, (128, VOC)))[:, :1]
    earlier = (named_col == named) & (row // 8 < lane // 8)
    rank = jnp.sum(jnp.where(earlier, 0.125, 0.0), axis=0, keepdims=True)
    wanted = (row // 16).astype(jnp.float32)
    place = (row // 8 % 2).astype(jnp.float32)
    chosen = (wanted == named) & (place == rank) & (row % 8 == lane % 8)
    pack[...] = jnp.where(chosen, 1.0, 0.0).astype(jnp.bfloat16)
    ids = jnp.broadcast_to(targets_ref[...].astype(jnp.float32), (128, TOK))
    tcol[...] = jnp.transpose(ids)

    def step0(n):
        relay_z(0, q0, n, x)
        send_x0(n)

    def step1(n):
        relay_z(1, q1, n, mine_x)
        send_y1(n)

    def finish0(n):
        for i in range(3):
            landed(hb.at[q0, order[n], streams[i + 1]], gx0, (i, n))
        cross(q0, 0, n)

    def finish1(n):
        for i in range(3):
            landed(hb.at[q1, order[n], mod(mine_x - 1 - i, NX)], gy1, (i, n))
        cross(q1, 1, n)

    for i in range(3):
        landed(hb.at[q1, z, streams[i + 1]], gx1, (i,))
    spread_z(1, q1, mine_x)
    cross(q1, 1, 0)
    for n in (3, 4, 1, 2):
        step0(n)
    for n in (3, 4, 1, 2):
        step1(n)
    finish0(0)
    for n in (5, 6, 7):
        step0(n)
    for n in (5, 6, 7):
        step1(n)
    for n in range(1, 8):
        finish0(n)
        finish1(n)

    def logits(first, last):
        for n in range(first, last):
            mirror = n if n in (0, 7) else (n + 1 if n % 2 else n - 1)
            for part in range(2):
                landed(hb.at[2 - 2 * c + part, order[n]], gcore, (part, mirror))
        count = last - first
        left = jnp.concatenate(
            [
                jnp.concatenate(
                    [hb[q, order[n]].reshape(64, QUART) for n in range(first, last)],
                    axis=0,
                )
                for q in range(4)
            ],
            axis=1,
        )
        product = lax.dot_general(
            left, w[...], NT_DIMS, preferred_element_type=jnp.float32
        )
        for i in range(count):
            lbuf[order[first + i]] = product[i * 64:(i + 1) * 64]

    w_in.wait()
    logits(0, 5)
    logits(5, 8)

    scores = lbuf[...].reshape(TOK, VOC)
    lane1 = lax.broadcasted_iota(jnp.int32, (1, VOC), 1)
    ids_row = (
        (sec * 64 + lane1 // 8) * 64 + ten * 8 + lane1 % 8
    ).astype(jnp.float32)
    hits = tcol[:, :1] == ids_row
    top1 = jnp.max(scores, axis=1, keepdims=True)
    total1 = jnp.sum(jnp.exp(scores - top1), axis=1, keepdims=True)
    picked1 = jnp.sum(jnp.where(hits, scores, 0.0), axis=1, keepdims=True)
    lanes = lax.broadcasted_iota(jnp.int32, (TOK, 128), 1)
    stats = jnp.where(lanes == 0, top1, jnp.where(lanes == 1, total1, picked1))
    stats = jnp.transpose(stats)
    mine3 = (stats[0:1], stats[1:2], stats[2:3])

    def triple(ref, i):
        return tuple(ref[i, :, n * TOK:(n + 1) * TOK] for n in range(3))

    def merge(mine, parts):
        best = functools.reduce(jnp.maximum, [p[0] for p in parts], mine[0])
        total = mine[1] * jnp.exp(mine[0] - best)
        picked = mine[2]
        for p in parts:
            total += p[1] * jnp.exp(p[0] - best)
            picked += p[2]
        return best, total, picked

    def share(mine, phase, got, count, device):
        for n in range(3):
            st_s[phase, :, n * TOK:(n + 1) * TOK] = mine[n]
        for i in range(1, count):
            push(st_s.at[phase], got.at[i - 1], bsem, (phase, i - 1), device(i))
        for i in range(1, count):
            landed(got.at[i - 1], bsem, (phase, i - 1))
        return merge(mine, [triple(got, i) for i in range(count - 1)])

    def rows8(best, total, picked):
        sub = lax.broadcasted_iota(jnp.int32, (8, TOK), 0)
        return jnp.where(sub == 0, best, jnp.where(sub == 1, total, picked))

    mine3 = share(mine3, 0, st_z, NZ, lambda i: at_z(mod(z + i, NZ)))
    mine3 = share(mine3, 1, st_x, NX, lambda i: at_x(mod(x + i, NX)))
    best, total, picked = share(
        mine3, 2, st_t, NT, lambda i: (sec, mod(ten + i, NT))
    )
    loss = jnp.broadcast_to(jnp.log(total) + best - picked, (8, TOK))
    loss_ref[...] = pltpu.roll(loss, TOK - sec * ROWS, 1)[:1, :ROWS]
    back_cols = jnp.transpose(
        jnp.concatenate(
            [rows8(best, 1.0 / total, picked), jnp.zeros((120, TOK), jnp.float32)], axis=0
        )
    )
    dl = jnp.exp(scores - back_cols[:, :1]) * back_cols[:, 1:2]
    dlb[...] = (dl - jnp.where(hits, 1.0, 0.0)).astype(jnp.bfloat16)

    half = TOK // 2
    theirs = pl.multiple_of((1 - c) * half, half)
    ours = pl.multiple_of(c * half, half)

    chunks = [
        ("y", mod(y + 2, NY)),
        ("x", 0),
        ("y", mod(y + 1, NY)),
        ("x", 1),
        ("y", mod(y + 3, NY)),
        ("y", y),
    ]
    slot = {0: 0, 2: 1, 4: 2, 5: 3}

    def buffers(p):
        kind, i = chunks[p]
        if kind == "y":
            return r0s.at[slot[p]], r0r.at[slot[p]], own.at[slot[p]]
        return r0sx.at[i], r0rx.at[i], ownx.at[i]

    def compute(p):
        kind, i = chunks[p]
        wide = WIDE if kind == "y" else CROSS
        lo = pl.multiple_of(i * WIDE, 128) if kind == "y" else NY * WIDE + i * CROSS
        give_ref, got_ref, keep_ref = buffers(p)
        cols = w[:, pl.ds(lo, wide)]
        give = jnp.dot(dlb[pl.ds(theirs, half), :], cols, preferred_element_type=jnp.float32)
        give_ref[...] = give.astype(jnp.bfloat16).reshape(4, NX, ROWS, wide)
        push(give_ref, got_ref, r0sem, (p,), other)
        keep = jnp.dot(dlb[pl.ds(ours, half), :], cols, preferred_element_type=jnp.float32)
        keep_ref[...] = keep.reshape(4, NX, ROWS, wide)

    def group(r):
        return mod(x + ROUNDS[r], NX)

    def send_over(r):
        to = at_y(mod(y + (1 if r % 2 == 0 else 3), NY))
        push(ys.at[0, :, group(r)], tr.at[r], trsem, (r,), to)

    def send_y(n, r):
        piece = own[n, :, group(r)]
        if (n == 1) == (r % 2 == 0):
            landed(tr.at[r], trsem, (r,))
            piece += tr[r].astype(jnp.float32)
        ys[n, :, group(r)] = piece.astype(jnp.bfloat16)
        to = at_y(mod(y + (1 if n == 1 else 3), NY))
        push(ys.at[n, :, group(r)], yr.at[n - 1, :, group(r)], ysem, (n - 1, r), to)

    def pass_on(p):
        kind, i = chunks[p]
        _, got_ref, keep_ref = buffers(p)
        landed(got_ref, r0sem, (p,))
        both = keep_ref[...] + got_ref[...].astype(jnp.float32)
        if p == 0:
            ys[0] = both.astype(jnp.bfloat16)
            send_over(0)
            send_over(1)
            return
        keep_ref[...] = both
        if kind == "x":
            xs[i] = both.astype(jnp.bfloat16)
            for n, dx in enumerate(DX):
                push(
                    xs.at[i, :, mod(x + dx, NX)], xr.at[i, n], xsem, (i, n),
                    at_x(mod(x + dx, NX)),
                )

    compute(0)
    compute(1)
    pass_on(0)
    packed = lax.dot_general(
        pack[...], dlb[...], NT_DIMS, preferred_element_type=jnp.float32
    )
    a2as[...] = packed.astype(jnp.bfloat16).reshape(NS, ROWS, TOK)

    def scatter(i, carry):
        to = mod(sec + i, NS)
        pltpu.make_async_remote_copy(
            src_ref=a2as.at[to],
            dst_ref=a2ar.at[sec],
            send_sem=asem.at[0],
            recv_sem=asem.at[1],
            device_id=(to, ten),
            device_id_type=MESH,
        ).start()
        return carry

    lax.fori_loop(1, NS, scatter, 0)
    compute(4)
    pass_on(1)
    send_over(2)
    send_over(3)
    compute(2)
    pass_on(4)
    send_y(2, 0)
    compute(3)
    pass_on(2)
    send_y(1, 0)
    send_y(2, 1)
    send_y(1, 1)
    compute(5)
    pass_on(3)
    pass_on(5)
    send_y(2, 2)
    send_y(1, 2)
    send_y(2, 3)
    send_y(1, 3)

    def gather_y(r):
        to = group(r)
        both = own[3, :, to]
        for n in range(2):
            landed(yr.at[n, :, to], ysem, (n, r))
            both += yr[n, :, to].astype(jnp.float32)
        if r < 3:
            x2s[:, to] = both.astype(jnp.bfloat16)
            push(x2s.at[:, to], x2r.at[r], x2sem, (r,), at_x(to))
        return both

    def gather_x():
        for j in range(2):
            for n in range(3):
                landed(xr.at[j, n], xsem, (j, n))
            got = ownx[j, :, x]
            for n in range(3):
                got += xr[j, n].astype(jnp.float32)
            for h in range(2):
                piece = got[:, :, h * NARROW:(h + 1) * NARROW]
                acc2[2 * j + h] = piece
                y2s[2 * j + h] = piece.astype(jnp.bfloat16)
        for n in range(3):
            to = mod(y + n + 1, NY)
            push(y2s.at[to], y2r.at[n], y2sem, (n,), at_y(to))

    def weight_grads(q):
        grads = jnp.dot(
            a2ar[...].reshape(NS * ROWS, TOK),
            hb[q].reshape(TOK, QUART),
            preferred_element_type=jnp.float32,
        )
        slots_ref[:, q * QUART:(q + 1) * QUART] = grads.astype(jnp.bfloat16)

    z_copies = []

    def send_sections(part, src, dst):
        for i in range(4):
            to = 4 * c + i
            copy = pltpu.make_async_remote_copy(
                src_ref=src.at[i],
                dst_ref=dst.at[mod(to - z, NZ)],
                send_sem=zsem.at[0, part, i],
                recv_sem=zsem.at[1, part, 0],
                device_id=at_z(to),
                device_id_type=MESH,
            )
            z_copies.append((to, copy))

            @pl.when(to != z)
            def _():
                copy.start()

    gather_y(0)
    gather_y(1)
    gather_x()
    gather_y(2)
    a2ar[sec] = a2as[sec]
    pltpu.make_async_copy(
        a2ar.at[pl.ds(0, NS - 1)], a2ar.at[pl.ds(0, NS - 1)], asem.at[1]
    ).wait()
    weight_grads(0)
    weight_grads(1)
    narrow = acc2[y]
    for n in range(3):
        landed(y2r.at[n], y2sem, (n,))
        narrow += y2r[n].astype(jnp.float32)
    zf[:, :, WIDE:] = narrow
    zsn[...] = narrow.astype(jnp.bfloat16)
    send_sections(1, zsn, zrn)
    wide = gather_y(3)
    for n in range(3):
        landed(x2r.at[n], x2sem, (n,))
        wide += x2r[n].astype(jnp.float32)
    zf[:, :, :WIDE] = wide
    zsw[...] = wide.astype(jnp.bfloat16)
    send_sections(0, zsw, zrw)
    weight_grads(2)
    weight_grads(3)
    mine = z // 4 == c

    f_copies = []
    for t in range(NT):
        copy = pltpu.make_async_remote_copy(
            src_ref=fin_s.at[t],
            dst_ref=fin_r.at[y],
            send_sem=fsem.at[0, t],
            recv_sem=fsem.at[1, y],
            device_id=(sec, jnp.int32(t)),
            device_id_type=MESH,
        )
        f_copies.append(copy)

    @pl.when(mine)
    def _():
        for part, got in enumerate((zrw, zrn)):
            pltpu.make_async_copy(
                got.at[pl.ds(1, NZ - 1)], got.at[pl.ds(1, NZ - 1)], zsem.at[1, part, 0]
            ).wait()
        high, low = zf[z % 4, :, :WIDE], zf[z % 4, :, WIDE:]
        for i in range(1, NZ):
            high += zrw[i].astype(jnp.float32)
            low += zrn[i].astype(jnp.float32)
        final = jnp.concatenate([high, low], axis=1)
        for t in range(NT):
            fin_s[t] = final[2 * t:2 * t + 2]
        for t in range(NT):
            @pl.when(ten != t)
            def _():
                f_copies[t].start()

        fin_r[y] = fin_s[ten]

    for i in range(NY):
        @pl.when(jnp.logical_not(mine & (y == i)))
        def _():
            landed(fin_r.at[i], fsem, (i,))

        hgrad_ref[:, i * WIDE:(i + 1) * WIDE] = fin_r[i, :, :WIDE]
        hgrad_ref[:, NY * WIDE + i * NARROW:NY * WIDE + (i + 1) * NARROW] = fin_r[
            i, :, WIDE:
        ]

    @pl.when(mine)
    def _():
        for t in range(NT):
            @pl.when(ten != t)
            def _():
                f_copies[t].wait_send()

    for to, copy in z_copies:
        @pl.when(to != z)
        def _():
            copy.wait_send()

    for copy in sent:
        copy.wait_send()
    pltpu.make_async_copy(
        a2as.at[pl.ds(0, NS - 1)], a2as.at[pl.ds(0, NS - 1)], asem.at[0]
    ).wait()


def on_device(hidden, head_weight, panel_section, targets):
    per_section, rows, width = head_weight.shape
    bf16, f32 = jnp.bfloat16, jnp.float32
    vmem = pl.BlockSpec(memory_space=pltpu.VMEM)
    hbm = pl.BlockSpec(memory_space=pltpu.HBM)
    dma = pltpu.SemaphoreType.DMA
    loss, hidden_grad, grads = pl.pallas_call(
        body,
        name="head_step",
        out_shape=(
            pltpu.VMEM((1, ROWS), f32),
            pltpu.VMEM((2, D), f32),
            pltpu.VMEM((NS * ROWS, D), bf16),
        ),
        in_specs=[hbm, hbm, hbm, hbm],
        out_specs=(vmem, vmem, vmem),
        scratch_shapes=[
            pltpu.VMEM((1, NS * 64), jnp.int32),
            pltpu.VMEM((1, TOK), jnp.int32),
            pltpu.VMEM((VOC, D), bf16),
            pltpu.VMEM((4, NZ, NX, ROWS, QUART), bf16),
            pltpu.VMEM((NZ, 64, VOC), f32),
            pltpu.VMEM((TOK, VOC), bf16),
            pltpu.VMEM((VOC, VOC), bf16),
            pltpu.VMEM((TOK, 128), f32),
            pltpu.VMEM((NS, ROWS, TOK), bf16),
            pltpu.VMEM((NS, ROWS, TOK), bf16),
            pltpu.VMEM((3, 1, 3 * TOK), f32),
            pltpu.VMEM((NZ - 1, 1, 3 * TOK), f32),
            pltpu.VMEM((NX - 1, 1, 3 * TOK), f32),
            pltpu.VMEM((NT - 1, 1, 3 * TOK), f32),
            pltpu.VMEM((4, 4, NX, ROWS, WIDE), bf16),
            pltpu.VMEM((4, 4, NX, ROWS, WIDE), bf16),
            pltpu.VMEM((4, 4, NX, ROWS, WIDE), f32),
            pltpu.VMEM((2, 4, NX, ROWS, CROSS), bf16),
            pltpu.VMEM((2, 4, NX, ROWS, CROSS), bf16),
            pltpu.VMEM((2, 4, NX, ROWS, CROSS), f32),
            pltpu.VMEM((4, 4, ROWS, WIDE), bf16),
            pltpu.VMEM((3, 4, NX, ROWS, WIDE), bf16),
            pltpu.VMEM((2, 4, NX, ROWS, WIDE), bf16),
            pltpu.VMEM((2, 4, NX, ROWS, CROSS), bf16),
            pltpu.VMEM((2, 3, 4, ROWS, CROSS), bf16),
            pltpu.VMEM((4, NX, ROWS, WIDE), bf16),
            pltpu.VMEM((3, 4, ROWS, WIDE), bf16),
            pltpu.VMEM((4, 4, ROWS, NARROW), f32),
            pltpu.VMEM((4, 4, ROWS, NARROW), bf16),
            pltpu.VMEM((3, 4, ROWS, NARROW), bf16),
            pltpu.VMEM((4, ROWS, QUART), f32),
            pltpu.VMEM((4, ROWS, WIDE), bf16),
            pltpu.VMEM((4, ROWS, NARROW), bf16),
            pltpu.VMEM((NZ, ROWS, WIDE), bf16),
            pltpu.VMEM((NZ, ROWS, NARROW), bf16),
            pltpu.VMEM((NT, 2, QUART), f32),
            pltpu.VMEM((NY, 2, QUART), f32),
            dma((5,)),
            dma((2, 2, 8)),
            dma((2, 3, 8)),
            dma((2, 3)),
            dma((2, 3, 8)),
            dma((2, 2, 8)),
            dma((2, 3, 7)),
            dma((2,)),
            dma((2, 6)),
            dma((2, 4)),
            dma((2, 2, 4)),
            dma((2, 2, 3)),
            dma((2, 3)),
            dma((2, 3)),
            dma((2, 2, 4)),
            dma((2, 8)),
        ],
        compiler_params=pltpu.CompilerParams(
            collective_id=0, has_side_effects=True, vmem_limit_bytes=48 * 2**20
        ),
    )(
        *(
            pltpu.with_memory_space_constraint(array, pltpu.HBM)
            for array in (
                hidden,
                head_weight.reshape(per_section * rows, width),
                panel_section.reshape(1, -1),
                targets.reshape(1, -1),
            )
        )
    )
    return (loss.reshape(ROWS), hidden_grad, grads.reshape(1, NS, 2, rows, width))


def solution(mesh):
    in_specs = (P("section", None), P("section", "tensor", None), P(), P())
    out_specs = (
        P("section"),
        P(("section", "tensor"), None),
        P("section", None, None, "tensor", None),
    )
    return jax.shard_map(
        on_device, mesh=mesh, in_specs=in_specs, out_specs=out_specs, check_vma=False
    )
```

```python
import functools

import jax
import jax.numpy as jnp
from jax import lax
from jax.experimental import pallas as pl
from jax.experimental.pallas import tpu as pltpu
from jax.sharding import PartitionSpec as P

MESH = pl.DeviceIdType.MESH
NZ, NX, NY, NC = 8, 4, 4, 2
NS, NT = NZ * NX, NY * NC
D = 4608
TOK = 512
ROWS = 16
VOC = 512
QUART = D // 4
PIECES = 4
PARTS = (1280, 1024)
WIDE = 896
CROSS = 512
NARROW = 256
DX = (1, 3, 2)
ROUNDS = (2, 1, 3, 0)
NT_DIMS = (((1,), (1,)), ((), ()))


def mod(a, n):
    return lax.rem(a + 2 * n, n)


def body(
    hidden_hbm,
    weight_hbm,
    panels_hbm,
    targets_hbm,
    loss_ref,
    hgrad_ref,
    slots_ref,
    panels_ref,
    targets_ref,
    w,
    ha,
    hb,
    lbuf,
    dlb,
    pack,
    tcol,
    a2as,
    a2ar,
    st_s,
    st_z,
    st_x,
    st_t,
    r0s,
    r0r,
    own,
    r0sx,
    r0rx,
    ownx,
    tr,
    ys,
    yr,
    xs,
    xr,
    x2s,
    x2r,
    acc2,
    y2s,
    y2r,
    zf,
    zsw,
    zsn,
    zrw,
    zrn,
    fin_s,
    fin_r,
    local_sem,
    gz,
    gx0,
    gx1,
    gy1,
    gcore,
    bsem,
    asem,
    r0sem,
    trsem,
    ysem,
    xsem,
    x2sem,
    y2sem,
    zsem,
    fsem,
):
    sec = lax.axis_index("section")
    ten = lax.axis_index("tensor")
    z, x = sec // NX, sec % NX
    y, c = ten // NC, ten % NC
    sgn = 1 - 2 * c
    hbs = (ha, hb)

    def at_z(zz):
        return (zz * NX + x, ten)

    def at_x(xx):
        return (z * NX + xx, ten)

    def at_y(yy):
        return (sec, yy * NC + c)

    other = (sec, y * NC + 1 - c)
    sent = []

    def push(src, dst, sems, where, dev):
        copy = pltpu.make_async_remote_copy(
            src_ref=src,
            dst_ref=dst,
            send_sem=sems.at[(0, *where)],
            recv_sem=sems.at[(1, *where)],
            device_id=dev,
            device_id_type=MESH,
        )
        copy.start()
        sent.append(copy)

    def drain(count):
        for copy in sent[:count]:
            copy.wait_send()
        del sent[:count]

    def landed(dst, sems, where):
        pltpu.make_async_copy(dst, dst, sems.at[(1, *where)]).wait()

    own_in = []
    for part in range(2):
        for core in range(2):
            lo = core * D // 2 + part * PARTS[0]
            copy = pltpu.make_async_copy(
                hidden_hbm.at[:, lo:lo + PARTS[part]],
                hbs[part].at[core, z, x],
                local_sem.at[1 + part],
            )
            own_in.append((core, copy))

            @pl.when(c == core)
            def _():
                copy.start()

    names_in = pltpu.make_async_copy(panels_hbm, panels_ref, local_sem.at[3])
    names_in.start()
    targets_in = pltpu.make_async_copy(targets_hbm, targets_ref, local_sem.at[4])
    targets_in.start()
    w_in = pltpu.make_async_copy(weight_hbm, w, local_sem.at[0])
    w_in.start()
    barrier = pltpu.get_barrier_semaphore()

    def greet_sections(i, carry):
        pl.semaphore_signal(
            barrier, inc=1, device_id=(mod(sec + i, NS), ten), device_id_type=MESH
        )
        return carry

    lax.fori_loop(1, NS, greet_sections, 0)

    def greet_tensors(i, carry):
        pl.semaphore_signal(
            barrier, inc=1, device_id=(sec, mod(ten + i, NT)), device_id_type=MESH
        )
        return carry

    lax.fori_loop(1, NT, greet_tensors, 0)
    for core, copy in own_in:
        @pl.when(c == core)
        def _():
            copy.wait()

    pl.semaphore_wait(barrier, NS - 1 + NT - 1)

    def back(k):
        return mod(z - k * sgn, NZ)

    def ahead(k):
        return mod(z + k * sgn, NZ)

    order = [z] + [back((n + 1) // 2) if n % 2 else ahead(n // 2) for n in range(1, 8)]
    streams = [x] + [mod(x - dx, NX) for dx in DX]
    mine_x = mod(x + y, NX)

    def send_z(part, n, xx, to, arrives):
        piece = hbs[part].at[c, order[n], xx]
        push(piece, piece, gz, (part, arrives), at_z(order[to]))

    def spread_z(part, xx):
        for to, arrives in ((2, 1), (1, 2), (4, 3), (3, 4)):
            send_z(part, 0, xx, to, arrives)

    def relay_z(part, n, xx):
        landed(hbs[part].at[c, order[n], xx], gz, (part, n))
        if n == 3:
            send_z(part, 3, xx, 2, 5)
            send_z(part, 3, xx, 4, 7)
        if n == 4:
            send_z(part, 4, xx, 1, 6)

    def send_x0(n):
        piece = ha.at[c, order[n], x]
        for i, dx in enumerate(DX):
            push(piece, piece, gx0, (i, n), at_x(mod(x + dx, NX)))

    def send_y1(n):
        piece = hb.at[c, order[n], mine_x]
        for i in range(3):
            push(piece, piece, gy1, (i, n), at_y(mod(y + 1 + i, NY)))

    def cross(part, n):
        piece = hbs[part].at[c, order[n]]
        push(piece, piece, gcore, (part, n), other)

    for i, dx in enumerate(DX):
        push(hb.at[c, z, x], hb.at[c, z, x], gx1, (i,), at_x(mod(x + dx, NX)))
    spread_z(0, x)
    send_x0(0)

    names_in.wait()
    targets_in.wait()
    lane = lax.broadcasted_iota(jnp.int32, (VOC, VOC), 1)
    row = lax.broadcasted_iota(jnp.int32, (VOC, VOC), 0)
    base = pl.multiple_of((sec // 2) * 128, 128)
    names = panels_ref[:, pl.ds(base, 128)].astype(jnp.float32)
    names = jnp.broadcast_to(names, (8, 128)).astype(jnp.bfloat16)
    spread = (
        lax.broadcasted_iota(jnp.int32, (128, VOC), 0)
        == lax.broadcasted_iota(jnp.int32, (128, VOC), 1) // 8 + (sec % 2) * 64
    )
    named = jnp.dot(
        names, spread.astype(jnp.float32).astype(jnp.bfloat16),
        preferred_element_type=jnp.float32,
    )[:1]
    named_col = jnp.transpose(jnp.broadcast_to(named, (128, VOC)))[:, :1]
    earlier = (named_col == named) & (row // 8 < lane // 8)
    rank = jnp.sum(jnp.where(earlier, 0.125, 0.0), axis=0, keepdims=True)
    wanted = (row // 16).astype(jnp.float32)
    place = (row // 8 % 2).astype(jnp.float32)
    chosen = (wanted == named) & (place == rank) & (row % 8 == lane % 8)
    pack[...] = jnp.where(chosen, 1.0, 0.0).astype(jnp.bfloat16)
    ids = jnp.broadcast_to(targets_ref[...].astype(jnp.float32), (128, TOK))
    tcol[...] = jnp.transpose(ids)

    def step0(n):
        relay_z(0, n, x)
        send_x0(n)

    def step1(n):
        relay_z(1, n, mine_x)
        send_y1(n)

    def finish0(n):
        for i in range(3):
            landed(ha.at[c, order[n], streams[i + 1]], gx0, (i, n))
        cross(0, n)

    def finish1(n):
        for i in range(3):
            landed(hb.at[c, order[n], mod(mine_x - 1 - i, NX)], gy1, (i, n))
        cross(1, n)

    for i in range(3):
        landed(hb.at[c, z, streams[i + 1]], gx1, (i,))
    spread_z(1, mine_x)
    cross(1, 0)
    for n in (3, 4, 1, 2):
        step0(n)
    for n in (3, 4, 1, 2):
        step1(n)
    finish0(0)
    for n in (5, 6, 7):
        step0(n)
    for n in (5, 6, 7):
        step1(n)
    for n in range(1, 8):
        finish0(n)
        finish1(n)

    def logits(first, last):
        for n in range(first, last):
            mirror = n if n in (0, 7) else (n + 1 if n % 2 else n - 1)
            for part in range(2):
                landed(hbs[part].at[1 - c, order[n]], gcore, (part, mirror))
        count = last - first
        left = jnp.concatenate(
            [
                jnp.concatenate(
                    [
                        hbs[part][core, order[n]].reshape(64, PARTS[part])
                        for n in range(first, last)
                    ],
                    axis=0,
                )
                for core in range(NC)
                for part in range(2)
            ],
            axis=1,
        )
        product = lax.dot_general(
            left, w[...], NT_DIMS, preferred_element_type=jnp.float32
        )
        for i in range(count):
            lbuf[order[first + i]] = product[i * 64:(i + 1) * 64]

    w_in.wait()
    logits(0, 5)
    logits(5, 8)

    scores = lbuf[...].reshape(TOK, VOC)
    lane1 = lax.broadcasted_iota(jnp.int32, (1, VOC), 1)
    ids_row = (
        (sec * 64 + lane1 // 8) * 64 + ten * 8 + lane1 % 8
    ).astype(jnp.float32)
    hits = tcol[:, :1] == ids_row
    top1 = jnp.max(scores, axis=1, keepdims=True)
    total1 = jnp.sum(jnp.exp(scores - top1), axis=1, keepdims=True)
    picked1 = jnp.sum(jnp.where(hits, scores, 0.0), axis=1, keepdims=True)
    lanes = lax.broadcasted_iota(jnp.int32, (TOK, 128), 1)
    stats = jnp.where(lanes == 0, top1, jnp.where(lanes == 1, total1, picked1))
    stats = jnp.transpose(stats)
    mine3 = (stats[0:1], stats[1:2], stats[2:3])

    def triple(ref, i):
        return tuple(ref[i, :, n * TOK:(n + 1) * TOK] for n in range(3))

    def merge(mine, parts):
        best = functools.reduce(jnp.maximum, [p[0] for p in parts], mine[0])
        total = mine[1] * jnp.exp(mine[0] - best)
        picked = mine[2]
        for p in parts:
            total += p[1] * jnp.exp(p[0] - best)
            picked += p[2]
        return best, total, picked

    def share(mine, phase, got, count, device):
        for n in range(3):
            st_s[phase, :, n * TOK:(n + 1) * TOK] = mine[n]
        for i in sorted(range(1, count), key=lambda i: abs(i - count // 2)):
            push(st_s.at[phase], got.at[i - 1], bsem, (phase, i - 1), device(i))
        for i in range(1, count):
            landed(got.at[i - 1], bsem, (phase, i - 1))
        return merge(mine, [triple(got, i) for i in range(count - 1)])

    def rows8(best, total, picked):
        sub = lax.broadcasted_iota(jnp.int32, (8, TOK), 0)
        return jnp.where(sub == 0, best, jnp.where(sub == 1, total, picked))

    mine3 = share(mine3, 0, st_z, NZ, lambda i: at_z(mod(z + i, NZ)))
    mine3 = share(mine3, 1, st_x, NX, lambda i: at_x(mod(x + i, NX)))
    best, total, picked = share(
        mine3, 2, st_t, NT, lambda i: (sec, mod(ten + i, NT))
    )
    back_cols = jnp.transpose(
        jnp.concatenate(
            [rows8(best, 1.0 / total, picked), jnp.zeros((120, TOK), jnp.float32)], axis=0
        )
    )
    dl = jnp.exp(scores - back_cols[:, :1]) * back_cols[:, 1:2]
    dlb[...] = (dl - jnp.where(hits, 1.0, 0.0)).astype(jnp.bfloat16)

    early = len(sent)
    half = TOK // 2
    theirs = pl.multiple_of((1 - c) * half, half)
    ours = pl.multiple_of(c * half, half)

    chunks = [
        ("y", mod(y + 2, NY)),
        ("x", 0),
        ("y", mod(y + 1, NY)),
        ("x", 1),
        ("y", mod(y + 3, NY)),
        ("y", y),
    ]
    slot = {0: 0, 2: 1, 4: 2, 5: 3}

    def buffers(p):
        kind, i = chunks[p]
        if kind == "y":
            return r0s.at[slot[p]], r0r.at[slot[p]], own.at[slot[p]]
        return r0sx.at[i], r0rx.at[i], ownx.at[i]

    def compute(p):
        kind, i = chunks[p]
        wide = WIDE if kind == "y" else CROSS
        lo = pl.multiple_of(i * WIDE, 128) if kind == "y" else NY * WIDE + i * CROSS
        give_ref, got_ref, keep_ref = buffers(p)
        cols = w[:, pl.ds(lo, wide)]
        give = jnp.dot(dlb[pl.ds(theirs, half), :], cols, preferred_element_type=jnp.float32)
        give_ref[...] = give.astype(jnp.bfloat16).reshape(4, NX, ROWS, wide)
        push(give_ref, got_ref, r0sem, (p,), other)
        keep = jnp.dot(dlb[pl.ds(ours, half), :], cols, preferred_element_type=jnp.float32)
        keep_ref[...] = keep.reshape(4, NX, ROWS, wide)

    def group(r):
        return mod(x + ROUNDS[r], NX)

    def send_over(r):
        to = at_y(mod(y + (1 if r % 2 == 0 else 3), NY))
        push(ys.at[0, :, group(r)], tr.at[r], trsem, (r,), to)

    def send_y(n, r):
        piece = own[n, :, group(r)]
        if (n == 1) == (r % 2 == 0):
            landed(tr.at[r], trsem, (r,))
            piece += tr[r].astype(jnp.float32)
        ys[n, :, group(r)] = piece.astype(jnp.bfloat16)
        to = at_y(mod(y + (1 if n == 1 else 3), NY))
        push(ys.at[n, :, group(r)], yr.at[n - 1, :, group(r)], ysem, (n - 1, r), to)

    def pass_on(p):
        kind, i = chunks[p]
        _, got_ref, keep_ref = buffers(p)
        landed(got_ref, r0sem, (p,))
        both = keep_ref[...] + got_ref[...].astype(jnp.float32)
        if p == 0:
            ys[0] = both.astype(jnp.bfloat16)
            send_over(0)
            send_over(1)
            return
        keep_ref[...] = both
        if kind == "x":
            xs[i] = both.astype(jnp.bfloat16)
            for n, dx in enumerate(DX):
                push(
                    xs.at[i, :, mod(x + dx, NX)], xr.at[i, n], xsem, (i, n),
                    at_x(mod(x + dx, NX)),
                )

    compute(0)
    compute(1)
    pass_on(0)
    packed = lax.dot_general(
        pack[...], dlb[...], NT_DIMS, preferred_element_type=jnp.float32
    )
    a2as[...] = packed.astype(jnp.bfloat16).reshape(NS, ROWS, TOK)

    def scatter(i, carry):
        to = mod(sec + i, NS)
        pltpu.make_async_remote_copy(
            src_ref=a2as.at[to],
            dst_ref=a2ar.at[sec],
            send_sem=asem.at[0],
            recv_sem=asem.at[1],
            device_id=(to, ten),
            device_id_type=MESH,
        ).start()
        return carry

    lax.fori_loop(1, NS, scatter, 0)
    compute(4)
    pass_on(1)
    send_over(2)
    send_over(3)
    compute(2)
    pass_on(4)
    send_y(2, 0)
    compute(3)
    pass_on(2)
    send_y(1, 0)
    send_y(2, 1)
    send_y(1, 1)
    compute(5)
    pass_on(3)
    pass_on(5)
    send_y(2, 2)
    send_y(1, 2)
    send_y(2, 3)
    send_y(1, 3)

    def gather_y(r):
        to = group(r)
        both = own[3, :, to]
        for n in range(2):
            landed(yr.at[n, :, to], ysem, (n, r))
            both += yr[n, :, to].astype(jnp.float32)
        if r < 3:
            x2s[:, to] = both.astype(jnp.bfloat16)
            push(x2s.at[:, to], x2r.at[r], x2sem, (r,), at_x(to))
        return both

    def gather_x():
        for j in range(2):
            for n in range(3):
                landed(xr.at[j, n], xsem, (j, n))
            got = ownx[j, :, x]
            for n in range(3):
                got += xr[j, n].astype(jnp.float32)
            for h in range(2):
                piece = got[:, :, h * NARROW:(h + 1) * NARROW]
                acc2[2 * j + h] = piece
                y2s[2 * j + h] = piece.astype(jnp.bfloat16)
        for n in range(3):
            to = mod(y + n + 1, NY)
            push(y2s.at[to], y2r.at[n], y2sem, (n,), at_y(to))

    def weight_grads(core, part):
        wide = PARTS[part]
        grads = jnp.dot(
            a2ar[...].reshape(NS * ROWS, TOK),
            hbs[part][core].reshape(TOK, wide),
            preferred_element_type=jnp.float32,
        )
        lo = core * D // 2 + part * PARTS[0]
        slots_ref[:, lo:lo + wide] = grads.astype(jnp.bfloat16)

    z_copies = []

    def send_sections(part, src, dst):
        for i in range(4):
            to = 4 * c + i
            copy = pltpu.make_async_remote_copy(
                src_ref=src.at[i],
                dst_ref=dst.at[mod(to - z, NZ)],
                send_sem=zsem.at[0, part, i],
                recv_sem=zsem.at[1, part, 0],
                device_id=at_z(to),
                device_id_type=MESH,
            )
            z_copies.append((to, copy))

            @pl.when(to != z)
            def _():
                copy.start()

    drain(early)
    loss = jnp.broadcast_to(jnp.log(total) + best - picked, (8, TOK))
    loss_ref[...] = pltpu.roll(loss, TOK - sec * ROWS, 1)[:1, :ROWS]
    gather_y(0)
    gather_y(1)
    gather_x()
    gather_y(2)
    a2ar[sec] = a2as[sec]
    pltpu.make_async_copy(
        a2ar.at[pl.ds(0, NS - 1)], a2ar.at[pl.ds(0, NS - 1)], asem.at[1]
    ).wait()
    weight_grads(0, 0)
    weight_grads(0, 1)
    narrow = acc2[y]
    for n in range(3):
        landed(y2r.at[n], y2sem, (n,))
        narrow += y2r[n].astype(jnp.float32)
    zf[:, :, WIDE:] = narrow
    zsn[...] = narrow.astype(jnp.bfloat16)
    send_sections(1, zsn, zrn)
    wide = gather_y(3)
    for n in range(3):
        landed(x2r.at[n], x2sem, (n,))
        wide += x2r[n].astype(jnp.float32)
    zf[:, :, :WIDE] = wide
    zsw[...] = wide.astype(jnp.bfloat16)
    send_sections(0, zsw, zrw)
    weight_grads(1, 0)
    weight_grads(1, 1)
    drain(len(sent))
    pltpu.make_async_copy(
        a2as.at[pl.ds(0, NS - 1)], a2as.at[pl.ds(0, NS - 1)], asem.at[0]
    ).wait()
    mine = z // 4 == c

    f_copies = []
    for t in range(NT):
        copy = pltpu.make_async_remote_copy(
            src_ref=fin_s.at[t],
            dst_ref=fin_r.at[y],
            send_sem=fsem.at[0, t],
            recv_sem=fsem.at[1, y],
            device_id=(sec, jnp.int32(t)),
            device_id_type=MESH,
        )
        f_copies.append(copy)

    @pl.when(mine)
    def _():
        for part, got in enumerate((zrw, zrn)):
            pltpu.make_async_copy(
                got.at[pl.ds(1, NZ - 1)], got.at[pl.ds(1, NZ - 1)], zsem.at[1, part, 0]
            ).wait()
        high, low = zf[z % 4, :, :WIDE], zf[z % 4, :, WIDE:]
        for i in range(1, NZ):
            high += zrw[i].astype(jnp.float32)
            low += zrn[i].astype(jnp.float32)
        final = jnp.concatenate([high, low], axis=1)
        for t in range(NT):
            fin_s[t] = final[2 * t:2 * t + 2]
        for t in range(NT):
            @pl.when(ten != t)
            def _():
                f_copies[t].start()

        fin_r[y] = fin_s[ten]

    for to, copy in z_copies:
        @pl.when(to != z)
        def _():
            copy.wait_send()

    for i in range(NY):
        @pl.when(jnp.logical_not(mine & (y == i)))
        def _():
            landed(fin_r.at[i], fsem, (i,))

        hgrad_ref[:, i * WIDE:(i + 1) * WIDE] = fin_r[i, :, :WIDE]
        hgrad_ref[:, NY * WIDE + i * NARROW:NY * WIDE + (i + 1) * NARROW] = fin_r[
            i, :, WIDE:
        ]

    @pl.when(mine)
    def _():
        for t in range(NT):
            @pl.when(ten != t)
            def _():
                f_copies[t].wait_send()


def write_out(loss_ref, hgrad_ref, slots_ref, loss_hbm, hgrad_hbm, slots_hbm, sems):
    rows = NS * ROWS // PIECES
    copies = [
        pltpu.make_async_copy(
            slots_ref.at[i * rows:(i + 1) * rows],
            slots_hbm.at[i * rows:(i + 1) * rows],
            sems.at[2 + i],
        )
        for i in range(PIECES)
    ]
    copies.append(pltpu.make_async_copy(loss_ref, loss_hbm, sems.at[0]))
    copies.append(pltpu.make_async_copy(hgrad_ref, hgrad_hbm, sems.at[1]))
    for copy in copies:
        copy.start()
    for copy in copies:
        copy.wait()


def on_device(hidden, head_weight, panel_section, targets):
    per_section, rows, width = head_weight.shape
    bf16, f32 = jnp.bfloat16, jnp.float32
    vmem = pl.BlockSpec(memory_space=pltpu.VMEM)
    hbm = pl.BlockSpec(memory_space=pltpu.HBM)
    dma = pltpu.SemaphoreType.DMA
    loss, hidden_grad, grads = pl.pallas_call(
        body,
        name="head_step",
        out_shape=(
            pltpu.VMEM((1, ROWS), f32),
            pltpu.VMEM((2, D), f32),
            pltpu.VMEM((NS * ROWS, D), bf16),
        ),
        in_specs=[hbm, hbm, hbm, hbm],
        out_specs=(vmem, vmem, vmem),
        scratch_shapes=[
            pltpu.VMEM((1, NS * 64), jnp.int32),
            pltpu.VMEM((1, TOK), jnp.int32),
            pltpu.VMEM((VOC, D), bf16),
            pltpu.VMEM((NC, NZ, NX, ROWS, PARTS[0]), bf16),
            pltpu.VMEM((NC, NZ, NX, ROWS, PARTS[1]), bf16),
            pltpu.VMEM((NZ, 64, VOC), f32),
            pltpu.VMEM((TOK, VOC), bf16),
            pltpu.VMEM((VOC, VOC), bf16),
            pltpu.VMEM((TOK, 128), f32),
            pltpu.VMEM((NS, ROWS, TOK), bf16),
            pltpu.VMEM((NS, ROWS, TOK), bf16),
            pltpu.VMEM((3, 1, 3 * TOK), f32),
            pltpu.VMEM((NZ - 1, 1, 3 * TOK), f32),
            pltpu.VMEM((NX - 1, 1, 3 * TOK), f32),
            pltpu.VMEM((NT - 1, 1, 3 * TOK), f32),
            pltpu.VMEM((4, 4, NX, ROWS, WIDE), bf16),
            pltpu.VMEM((4, 4, NX, ROWS, WIDE), bf16),
            pltpu.VMEM((4, 4, NX, ROWS, WIDE), f32),
            pltpu.VMEM((2, 4, NX, ROWS, CROSS), bf16),
            pltpu.VMEM((2, 4, NX, ROWS, CROSS), bf16),
            pltpu.VMEM((2, 4, NX, ROWS, CROSS), f32),
            pltpu.VMEM((4, 4, ROWS, WIDE), bf16),
            pltpu.VMEM((3, 4, NX, ROWS, WIDE), bf16),
            pltpu.VMEM((2, 4, NX, ROWS, WIDE), bf16),
            pltpu.VMEM((2, 4, NX, ROWS, CROSS), bf16),
            pltpu.VMEM((2, 3, 4, ROWS, CROSS), bf16),
            pltpu.VMEM((4, NX, ROWS, WIDE), bf16),
            pltpu.VMEM((3, 4, ROWS, WIDE), bf16),
            pltpu.VMEM((4, 4, ROWS, NARROW), f32),
            pltpu.VMEM((4, 4, ROWS, NARROW), bf16),
            pltpu.VMEM((3, 4, ROWS, NARROW), bf16),
            pltpu.VMEM((4, ROWS, QUART), f32),
            pltpu.VMEM((4, ROWS, WIDE), bf16),
            pltpu.VMEM((4, ROWS, NARROW), bf16),
            pltpu.VMEM((NZ, ROWS, WIDE), bf16),
            pltpu.VMEM((NZ, ROWS, NARROW), bf16),
            pltpu.VMEM((NT, 2, QUART), f32),
            pltpu.VMEM((NY, 2, QUART), f32),
            dma((5,)),
            dma((2, 2, 8)),
            dma((2, 3, 8)),
            dma((2, 3)),
            dma((2, 3, 8)),
            dma((2, 2, 8)),
            dma((2, 3, 7)),
            dma((2,)),
            dma((2, 6)),
            dma((2, 4)),
            dma((2, 2, 4)),
            dma((2, 2, 3)),
            dma((2, 3)),
            dma((2, 3)),
            dma((2, 2, 4)),
            dma((2, 8)),
        ],
        compiler_params=pltpu.CompilerParams(
            collective_id=0, has_side_effects=True, vmem_limit_bytes=48 * 2**20
        ),
    )(
        *(
            pltpu.with_memory_space_constraint(array, pltpu.HBM)
            for array in (
                hidden,
                head_weight.reshape(per_section * rows, width),
                panel_section.reshape(1, -1),
                targets.reshape(1, -1),
            )
        )
    )
    loss, hidden_grad, grads = pl.pallas_call(
        write_out,
        name="write_out",
        out_shape=(
            jax.ShapeDtypeStruct((1, ROWS), f32),
            jax.ShapeDtypeStruct((2, D), f32),
            jax.ShapeDtypeStruct((NS * ROWS, D), bf16),
        ),
        in_specs=[vmem] * 3,
        out_specs=(hbm, hbm, hbm),
        scratch_shapes=[dma((2 + PIECES,))],
        compiler_params=pltpu.CompilerParams(vmem_limit_bytes=2 * 2**20),
    )(
        *(
            pltpu.with_memory_space_constraint(array, pltpu.VMEM)
            for array in (loss, hidden_grad, grads)
        )
    )
    return (loss.reshape(ROWS), hidden_grad, grads.reshape(1, NS, 2, rows, width))


def solution(mesh):
    in_specs = (P("section", None), P("section", "tensor", None), P(), P())
    out_specs = (
        P("section"),
        P(("section", "tensor"), None),
        P("section", None, None, "tensor", None),
    )
    return jax.shard_map(
        on_device, mesh=mesh, in_specs=in_specs, out_specs=out_specs, check_vma=False
    )
```

```python
import functools

import jax
import jax.numpy as jnp
from jax import lax
from jax.experimental import pallas as pl
from jax.experimental.pallas import tpu as pltpu
from jax.sharding import PartitionSpec as P

MESH = pl.DeviceIdType.MESH
NZ, NX, NY, NC = 8, 4, 4, 2
NS, NT = NZ * NX, NY * NC
D = 4608
TOK = 512
ROWS = 16
VOC = 512
QUART = D // 4
PIECES = 4
PARTS = (1280, 1024)
WIDE = 896
CROSS = 512
NARROW = 256
DX = (1, 3, 2)
ROUNDS = (2, 1, 3, 0)
NT_DIMS = (((1,), (1,)), ((), ()))


def mod(a, n):
    return lax.rem(a + 2 * n, n)


def body(
    hidden_hbm,
    weight_hbm,
    panels_hbm,
    targets_hbm,
    loss_ref,
    hgrad_ref,
    slots_ref,
    panels_ref,
    targets_ref,
    w,
    ha,
    hb,
    lbuf,
    dlb,
    pack,
    tcol,
    a2as,
    a2ar,
    st_s,
    st_z,
    st_x,
    st_t,
    r0s,
    r0r,
    own,
    r0sx,
    r0rx,
    ownx,
    tr,
    ys,
    yr,
    xs,
    xr,
    x2s,
    x2r,
    acc2,
    y2s,
    y2r,
    zf,
    zsw,
    zsn,
    zrw,
    zrn,
    fin_s,
    fin_r,
    local_sem,
    gz,
    gx0,
    gx1,
    gy1,
    gcore,
    bsem,
    asem,
    r0sem,
    trsem,
    ysem,
    xsem,
    x2sem,
    y2sem,
    zsem,
    fsem,
):
    sec = lax.axis_index("section")
    ten = lax.axis_index("tensor")
    z, x = sec // NX, sec % NX
    y, c = ten // NC, ten % NC
    sgn = 1 - 2 * c
    hbs = (ha, hb)

    def at_z(zz):
        return (zz * NX + x, ten)

    def at_x(xx):
        return (z * NX + xx, ten)

    def at_y(yy):
        return (sec, yy * NC + c)

    other = (sec, y * NC + 1 - c)
    sent = []

    def push(src, dst, sems, where, dev):
        copy = pltpu.make_async_remote_copy(
            src_ref=src,
            dst_ref=dst,
            send_sem=sems.at[(0, *where)],
            recv_sem=sems.at[(1, *where)],
            device_id=dev,
            device_id_type=MESH,
        )
        copy.start()
        sent.append(copy)

    def drain(count):
        for copy in sent[:count]:
            copy.wait_send()
        del sent[:count]

    def landed(dst, sems, where):
        pltpu.make_async_copy(dst, dst, sems.at[(1, *where)]).wait()

    own_in = []
    for part in range(2):
        for core in range(2):
            lo = core * D // 2 + part * PARTS[0]
            copy = pltpu.make_async_copy(
                hidden_hbm.at[:, lo:lo + PARTS[part]],
                hbs[part].at[core, z, x],
                local_sem.at[1 + part],
            )
            own_in.append((core, copy))

            @pl.when(c == core)
            def _():
                copy.start()

    names_in = pltpu.make_async_copy(panels_hbm, panels_ref, local_sem.at[3])
    names_in.start()
    targets_in = pltpu.make_async_copy(targets_hbm, targets_ref, local_sem.at[4])
    targets_in.start()
    w_in = pltpu.make_async_copy(weight_hbm, w, local_sem.at[0])
    w_in.start()
    barrier = pltpu.get_barrier_semaphore()

    def greet_sections(i, carry):
        pl.semaphore_signal(
            barrier, inc=1, device_id=(mod(sec + i, NS), ten), device_id_type=MESH
        )
        return carry

    lax.fori_loop(1, NS, greet_sections, 0)

    def greet_tensors(i, carry):
        pl.semaphore_signal(
            barrier, inc=1, device_id=(sec, mod(ten + i, NT)), device_id_type=MESH
        )
        return carry

    lax.fori_loop(1, NT, greet_tensors, 0)
    for core, copy in own_in:
        @pl.when(c == core)
        def _():
            copy.wait()

    pl.semaphore_wait(barrier, NS - 1 + NT - 1)

    def back(k):
        return mod(z - k * sgn, NZ)

    def ahead(k):
        return mod(z + k * sgn, NZ)

    order = [z] + [back((n + 1) // 2) if n % 2 else ahead(n // 2) for n in range(1, 8)]
    streams = [x] + [mod(x - dx, NX) for dx in DX]
    mine_x = mod(x + y, NX)

    def send_z(part, n, xx, to, arrives):
        piece = hbs[part].at[c, order[n], xx]
        push(piece, piece, gz, (part, arrives), at_z(order[to]))

    def spread_z(part, xx):
        for to, arrives in ((2, 1), (1, 2), (4, 3), (3, 4)):
            send_z(part, 0, xx, to, arrives)

    def relay_z(part, n, xx):
        landed(hbs[part].at[c, order[n], xx], gz, (part, n))
        if n == 3:
            send_z(part, 3, xx, 2, 5)
            send_z(part, 3, xx, 4, 7)
        if n == 4:
            send_z(part, 4, xx, 1, 6)

    def send_x0(n):
        piece = ha.at[c, order[n], x]
        for i, dx in enumerate(DX):
            push(piece, piece, gx0, (i, n), at_x(mod(x + dx, NX)))

    def send_y1(n):
        piece = hb.at[c, order[n], mine_x]
        for i in range(3):
            push(piece, piece, gy1, (i, n), at_y(mod(y + 1 + i, NY)))

    def cross(part, n):
        piece = hbs[part].at[c, order[n]]
        push(piece, piece, gcore, (part, n), other)

    for i, dx in enumerate(DX):
        push(hb.at[c, z, x], hb.at[c, z, x], gx1, (i,), at_x(mod(x + dx, NX)))
    spread_z(0, x)
    send_x0(0)

    names_in.wait()
    targets_in.wait()
    lane = lax.broadcasted_iota(jnp.int32, (VOC, VOC), 1)
    row = lax.broadcasted_iota(jnp.int32, (VOC, VOC), 0)
    base = pl.multiple_of((sec // 2) * 128, 128)
    names = panels_ref[:, pl.ds(base, 128)].astype(jnp.float32)
    names = jnp.broadcast_to(names, (8, 128)).astype(jnp.bfloat16)
    spread = (
        lax.broadcasted_iota(jnp.int32, (128, VOC), 0)
        == lax.broadcasted_iota(jnp.int32, (128, VOC), 1) // 8 + (sec % 2) * 64
    )
    named = jnp.dot(
        names, spread.astype(jnp.float32).astype(jnp.bfloat16),
        preferred_element_type=jnp.float32,
    )[:1]
    named_col = jnp.transpose(jnp.broadcast_to(named, (128, VOC)))[:, :1]
    earlier = (named_col == named) & (row // 8 < lane // 8)
    rank = jnp.sum(jnp.where(earlier, 0.125, 0.0), axis=0, keepdims=True)
    wanted = (row // 16).astype(jnp.float32)
    place = (row // 8 % 2).astype(jnp.float32)
    chosen = (wanted == named) & (place == rank) & (row % 8 == lane % 8)
    pack[...] = jnp.where(chosen, 1.0, 0.0).astype(jnp.bfloat16)
    ids = jnp.broadcast_to(targets_ref[...].astype(jnp.float32), (128, TOK))
    tcol[...] = jnp.transpose(ids)

    def step0(n):
        relay_z(0, n, x)
        send_x0(n)

    def step1(n):
        relay_z(1, n, mine_x)
        send_y1(n)

    def finish0(n):
        for i in range(3):
            landed(ha.at[c, order[n], streams[i + 1]], gx0, (i, n))
        cross(0, n)

    def finish1(n):
        for i in range(3):
            landed(hb.at[c, order[n], mod(mine_x - 1 - i, NX)], gy1, (i, n))
        cross(1, n)

    for i in range(3):
        landed(hb.at[c, z, streams[i + 1]], gx1, (i,))
    spread_z(1, mine_x)
    cross(1, 0)
    for n in (3, 4, 1, 2):
        step0(n)
    for n in (3, 4, 1, 2):
        step1(n)
    finish0(0)
    for n in (5, 6, 7):
        step0(n)
    for n in (5, 6, 7):
        step1(n)
    for n in range(1, 8):
        finish0(n)
        finish1(n)

    def logits(first, last):
        for n in range(first, last):
            mirror = n if n in (0, 7) else (n + 1 if n % 2 else n - 1)
            for part in range(2):
                landed(hbs[part].at[1 - c, order[n]], gcore, (part, mirror))
        count = last - first
        left = jnp.concatenate(
            [
                jnp.concatenate(
                    [
                        hbs[part][core, order[n]].reshape(64, PARTS[part])
                        for n in range(first, last)
                    ],
                    axis=0,
                )
                for core in range(NC)
                for part in range(2)
            ],
            axis=1,
        )
        product = lax.dot_general(
            left, w[...], NT_DIMS, preferred_element_type=jnp.float32
        )
        for i in range(count):
            lbuf[order[first + i]] = product[i * 64:(i + 1) * 64]

    w_in.wait()
    logits(0, 5)
    logits(5, 8)

    scores = lbuf[...].reshape(TOK, VOC)
    lane1 = lax.broadcasted_iota(jnp.int32, (1, VOC), 1)
    ids_row = (
        (sec * 64 + lane1 // 8) * 64 + ten * 8 + lane1 % 8
    ).astype(jnp.float32)
    hits = tcol[:, :1] == ids_row
    top1 = jnp.max(scores, axis=1, keepdims=True)
    total1 = jnp.sum(jnp.exp(scores - top1), axis=1, keepdims=True)
    picked1 = jnp.sum(jnp.where(hits, scores, 0.0), axis=1, keepdims=True)
    lanes = lax.broadcasted_iota(jnp.int32, (TOK, 128), 1)
    stats = jnp.where(lanes == 0, top1, jnp.where(lanes == 1, total1, picked1))
    stats = jnp.transpose(stats)
    mine3 = (stats[0:1], stats[1:2], stats[2:3])

    def triple(ref, i):
        return tuple(ref[i, :, n * TOK:(n + 1) * TOK] for n in range(3))

    def merge(mine, parts):
        best = functools.reduce(jnp.maximum, [p[0] for p in parts], mine[0])
        total = mine[1] * jnp.exp(mine[0] - best)
        picked = mine[2]
        for p in parts:
            total += p[1] * jnp.exp(p[0] - best)
            picked += p[2]
        return best, total, picked

    def share(mine, phase, got, count, device):
        for n in range(3):
            st_s[phase, :, n * TOK:(n + 1) * TOK] = mine[n]
        for i in sorted(range(1, count), key=lambda i: abs(i - count // 2)):
            push(st_s.at[phase], got.at[i - 1], bsem, (phase, i - 1), device(i))
        for i in range(1, count):
            landed(got.at[i - 1], bsem, (phase, i - 1))
        return merge(mine, [triple(got, i) for i in range(count - 1)])

    def rows8(best, total, picked):
        sub = lax.broadcasted_iota(jnp.int32, (8, TOK), 0)
        return jnp.where(sub == 0, best, jnp.where(sub == 1, total, picked))

    mine3 = share(mine3, 0, st_z, NZ, lambda i: at_z(mod(z + i, NZ)))
    mine3 = share(mine3, 1, st_x, NX, lambda i: at_x(mod(x + i, NX)))
    best, total, picked = share(
        mine3, 2, st_t, NT, lambda i: (sec, mod(ten + i, NT))
    )
    back_cols = jnp.transpose(
        jnp.concatenate(
            [rows8(best, 1.0 / total, picked), jnp.zeros((120, TOK), jnp.float32)], axis=0
        )
    )
    dl = jnp.exp(scores - back_cols[:, :1]) * back_cols[:, 1:2]
    dlb[...] = (dl - jnp.where(hits, 1.0, 0.0)).astype(jnp.bfloat16)

    early = len(sent)
    half = TOK // 2
    theirs = pl.multiple_of((1 - c) * half, half)
    ours = pl.multiple_of(c * half, half)

    chunks = [
        ("y", mod(y + 2, NY)),
        ("x", 0),
        ("y", mod(y + 1, NY)),
        ("x", 1),
        ("y", mod(y + 3, NY)),
        ("y", y),
    ]
    slot = {0: 0, 2: 1, 4: 2, 5: 3}

    def buffers(p):
        kind, i = chunks[p]
        if kind == "y":
            return r0s.at[slot[p]], r0r.at[slot[p]], own.at[slot[p]]
        return r0sx.at[i], r0rx.at[i], ownx.at[i]

    def compute(p):
        kind, i = chunks[p]
        wide = WIDE if kind == "y" else CROSS
        lo = pl.multiple_of(i * WIDE, 128) if kind == "y" else NY * WIDE + i * CROSS
        give_ref, got_ref, keep_ref = buffers(p)
        cols = w[:, pl.ds(lo, wide)]
        give = jnp.dot(dlb[pl.ds(theirs, half), :], cols, preferred_element_type=jnp.float32)
        give_ref[...] = give.astype(jnp.bfloat16).reshape(4, NX, ROWS, wide)
        push(give_ref, got_ref, r0sem, (p,), other)
        keep = jnp.dot(dlb[pl.ds(ours, half), :], cols, preferred_element_type=jnp.float32)
        keep_ref[...] = keep.reshape(4, NX, ROWS, wide)

    def group(r):
        return mod(x + ROUNDS[r], NX)

    def send_over(r):
        to = at_y(mod(y + (1 if r % 2 == 0 else 3), NY))
        push(ys.at[0, :, group(r)], tr.at[r], trsem, (r,), to)

    def send_y(n, r):
        piece = own[n, :, group(r)]
        if (n == 1) == (r % 2 == 0):
            landed(tr.at[r], trsem, (r,))
            piece += tr[r].astype(jnp.float32)
        ys[n, :, group(r)] = piece.astype(jnp.bfloat16)
        to = at_y(mod(y + (1 if n == 1 else 3), NY))
        push(ys.at[n, :, group(r)], yr.at[n - 1, :, group(r)], ysem, (n - 1, r), to)

    def pass_on(p):
        kind, i = chunks[p]
        _, got_ref, keep_ref = buffers(p)
        landed(got_ref, r0sem, (p,))
        both = keep_ref[...] + got_ref[...].astype(jnp.float32)
        if p == 0:
            ys[0] = both.astype(jnp.bfloat16)
            send_over(0)
            send_over(1)
            return
        keep_ref[...] = both
        if kind == "x":
            xs[i] = both.astype(jnp.bfloat16)
            for n, dx in enumerate(DX):
                push(
                    xs.at[i, :, mod(x + dx, NX)], xr.at[i, n], xsem, (i, n),
                    at_x(mod(x + dx, NX)),
                )

    compute(0)
    packed = lax.dot_general(
        pack[...], dlb[...], NT_DIMS, preferred_element_type=jnp.float32
    )
    a2as[...] = packed.astype(jnp.bfloat16).reshape(NS, ROWS, TOK)

    def scatter(i, carry):
        to = mod(sec + i, NS)
        pltpu.make_async_remote_copy(
            src_ref=a2as.at[to],
            dst_ref=a2ar.at[sec],
            send_sem=asem.at[0],
            recv_sem=asem.at[1],
            device_id=(to, ten),
            device_id_type=MESH,
        ).start()
        return carry

    lax.fori_loop(1, NS, scatter, 0)
    compute(1)
    pass_on(0)
    compute(4)
    pass_on(1)
    send_over(2)
    send_over(3)
    compute(2)
    pass_on(4)
    send_y(2, 0)
    compute(3)
    pass_on(2)
    send_y(1, 0)
    send_y(2, 1)
    send_y(1, 1)
    compute(5)
    pass_on(3)
    pass_on(5)
    send_y(2, 2)
    send_y(1, 2)
    send_y(2, 3)
    send_y(1, 3)

    def gather_y(r):
        to = group(r)
        both = own[3, :, to]
        for n in range(2):
            landed(yr.at[n, :, to], ysem, (n, r))
            both += yr[n, :, to].astype(jnp.float32)
        if r < 3:
            x2s[:, to] = both.astype(jnp.bfloat16)
            push(x2s.at[:, to], x2r.at[r], x2sem, (r,), at_x(to))
        return both

    def gather_x():
        for j in range(2):
            for n in range(3):
                landed(xr.at[j, n], xsem, (j, n))
            got = ownx[j, :, x]
            for n in range(3):
                got += xr[j, n].astype(jnp.float32)
            for h in range(2):
                piece = got[:, :, h * NARROW:(h + 1) * NARROW]
                acc2[2 * j + h] = piece
                y2s[2 * j + h] = piece.astype(jnp.bfloat16)
        for n in range(3):
            to = mod(y + n + 1, NY)
            push(y2s.at[to], y2r.at[n], y2sem, (n,), at_y(to))

    def weight_grads(core, part):
        wide = PARTS[part]
        grads = jnp.dot(
            a2ar[...].reshape(NS * ROWS, TOK),
            hbs[part][core].reshape(TOK, wide),
            preferred_element_type=jnp.float32,
        )
        lo = core * D // 2 + part * PARTS[0]
        slots_ref[:, lo:lo + wide] = grads.astype(jnp.bfloat16)

    z_copies = []

    def send_sections(part, src, dst):
        for i in range(4):
            to = 4 * c + i
            copy = pltpu.make_async_remote_copy(
                src_ref=src.at[i],
                dst_ref=dst.at[mod(to - z, NZ)],
                send_sem=zsem.at[0, part, i],
                recv_sem=zsem.at[1, part, 0],
                device_id=at_z(to),
                device_id_type=MESH,
            )
            z_copies.append((to, copy))

            @pl.when(to != z)
            def _():
                copy.start()

    drain(early)
    loss = jnp.broadcast_to(jnp.log(total) + best - picked, (8, TOK))
    loss_ref[...] = pltpu.roll(loss, TOK - sec * ROWS, 1)[:1, :ROWS]
    gather_y(0)
    gather_y(1)
    gather_x()
    gather_y(2)
    a2ar[sec] = a2as[sec]
    pltpu.make_async_copy(
        a2ar.at[pl.ds(0, NS - 1)], a2ar.at[pl.ds(0, NS - 1)], asem.at[1]
    ).wait()
    weight_grads(0, 0)
    weight_grads(0, 1)
    narrow = acc2[y]
    for n in range(3):
        landed(y2r.at[n], y2sem, (n,))
        narrow += y2r[n].astype(jnp.float32)
    zf[:, :, WIDE:] = narrow
    zsn[...] = narrow.astype(jnp.bfloat16)
    send_sections(1, zsn, zrn)
    wide = gather_y(3)
    for n in range(3):
        landed(x2r.at[n], x2sem, (n,))
        wide += x2r[n].astype(jnp.float32)
    zf[:, :, :WIDE] = wide
    zsw[...] = wide.astype(jnp.bfloat16)
    send_sections(0, zsw, zrw)
    weight_grads(1, 0)
    weight_grads(1, 1)
    drain(len(sent))
    pltpu.make_async_copy(
        a2as.at[pl.ds(0, NS - 1)], a2as.at[pl.ds(0, NS - 1)], asem.at[0]
    ).wait()
    mine = z // 4 == c

    f_copies = []
    for t in range(NT):
        copy = pltpu.make_async_remote_copy(
            src_ref=fin_s.at[t],
            dst_ref=fin_r.at[y],
            send_sem=fsem.at[0, t],
            recv_sem=fsem.at[1, y],
            device_id=(sec, jnp.int32(t)),
            device_id_type=MESH,
        )
        f_copies.append(copy)

    @pl.when(mine)
    def _():
        for part, got in enumerate((zrw, zrn)):
            pltpu.make_async_copy(
                got.at[pl.ds(1, NZ - 1)], got.at[pl.ds(1, NZ - 1)], zsem.at[1, part, 0]
            ).wait()
        high, low = zf[z % 4, :, :WIDE], zf[z % 4, :, WIDE:]
        for i in range(1, NZ):
            high += zrw[i].astype(jnp.float32)
            low += zrn[i].astype(jnp.float32)
        final = jnp.concatenate([high, low], axis=1)
        for t in range(NT):
            fin_s[t] = final[2 * t:2 * t + 2]
        for t in range(NT):
            @pl.when(ten != t)
            def _():
                f_copies[t].start()

        fin_r[y] = fin_s[ten]

    for to, copy in z_copies:
        @pl.when(to != z)
        def _():
            copy.wait_send()

    for i in range(NY):
        @pl.when(jnp.logical_not(mine & (y == i)))
        def _():
            landed(fin_r.at[i], fsem, (i,))

        hgrad_ref[:, i * WIDE:(i + 1) * WIDE] = fin_r[i, :, :WIDE]
        hgrad_ref[:, NY * WIDE + i * NARROW:NY * WIDE + (i + 1) * NARROW] = fin_r[
            i, :, WIDE:
        ]

    @pl.when(mine)
    def _():
        for t in range(NT):
            @pl.when(ten != t)
            def _():
                f_copies[t].wait_send()


def write_out(loss_ref, hgrad_ref, slots_ref, loss_hbm, hgrad_hbm, slots_hbm, sems):
    rows = NS * ROWS // PIECES
    copies = [
        pltpu.make_async_copy(
            slots_ref.at[i * rows:(i + 1) * rows],
            slots_hbm.at[i * rows:(i + 1) * rows],
            sems.at[2 + i],
        )
        for i in range(PIECES)
    ]
    copies.append(pltpu.make_async_copy(loss_ref, loss_hbm, sems.at[0]))
    copies.append(pltpu.make_async_copy(hgrad_ref, hgrad_hbm, sems.at[1]))
    for copy in copies:
        copy.start()
    for copy in copies:
        copy.wait()


def on_device(hidden, head_weight, panel_section, targets):
    per_section, rows, width = head_weight.shape
    bf16, f32 = jnp.bfloat16, jnp.float32
    vmem = pl.BlockSpec(memory_space=pltpu.VMEM)
    hbm = pl.BlockSpec(memory_space=pltpu.HBM)
    dma = pltpu.SemaphoreType.DMA
    loss, hidden_grad, grads = pl.pallas_call(
        body,
        name="head_step",
        out_shape=(
            pltpu.VMEM((1, ROWS), f32),
            pltpu.VMEM((2, D), f32),
            pltpu.VMEM((NS * ROWS, D), bf16),
        ),
        in_specs=[hbm, hbm, hbm, hbm],
        out_specs=(vmem, vmem, vmem),
        scratch_shapes=[
            pltpu.VMEM((1, NS * 64), jnp.int32),
            pltpu.VMEM((1, TOK), jnp.int32),
            pltpu.VMEM((VOC, D), bf16),
            pltpu.VMEM((NC, NZ, NX, ROWS, PARTS[0]), bf16),
            pltpu.VMEM((NC, NZ, NX, ROWS, PARTS[1]), bf16),
            pltpu.VMEM((NZ, 64, VOC), f32),
            pltpu.VMEM((TOK, VOC), bf16),
            pltpu.VMEM((VOC, VOC), bf16),
            pltpu.VMEM((TOK, 128), f32),
            pltpu.VMEM((NS, ROWS, TOK), bf16),
            pltpu.VMEM((NS, ROWS, TOK), bf16),
            pltpu.VMEM((3, 1, 3 * TOK), f32),
            pltpu.VMEM((NZ - 1, 1, 3 * TOK), f32),
            pltpu.VMEM((NX - 1, 1, 3 * TOK), f32),
            pltpu.VMEM((NT - 1, 1, 3 * TOK), f32),
            pltpu.VMEM((4, 4, NX, ROWS, WIDE), bf16),
            pltpu.VMEM((4, 4, NX, ROWS, WIDE), bf16),
            pltpu.VMEM((4, 4, NX, ROWS, WIDE), f32),
            pltpu.VMEM((2, 4, NX, ROWS, CROSS), bf16),
            pltpu.VMEM((2, 4, NX, ROWS, CROSS), bf16),
            pltpu.VMEM((2, 4, NX, ROWS, CROSS), f32),
            pltpu.VMEM((4, 4, ROWS, WIDE), bf16),
            pltpu.VMEM((3, 4, NX, ROWS, WIDE), bf16),
            pltpu.VMEM((2, 4, NX, ROWS, WIDE), bf16),
            pltpu.VMEM((2, 4, NX, ROWS, CROSS), bf16),
            pltpu.VMEM((2, 3, 4, ROWS, CROSS), bf16),
            pltpu.VMEM((4, NX, ROWS, WIDE), bf16),
            pltpu.VMEM((3, 4, ROWS, WIDE), bf16),
            pltpu.VMEM((4, 4, ROWS, NARROW), f32),
            pltpu.VMEM((4, 4, ROWS, NARROW), bf16),
            pltpu.VMEM((3, 4, ROWS, NARROW), bf16),
            pltpu.VMEM((4, ROWS, QUART), f32),
            pltpu.VMEM((4, ROWS, WIDE), bf16),
            pltpu.VMEM((4, ROWS, NARROW), bf16),
            pltpu.VMEM((NZ, ROWS, WIDE), bf16),
            pltpu.VMEM((NZ, ROWS, NARROW), bf16),
            pltpu.VMEM((NT, 2, QUART), f32),
            pltpu.VMEM((NY, 2, QUART), f32),
            dma((5,)),
            dma((2, 2, 8)),
            dma((2, 3, 8)),
            dma((2, 3)),
            dma((2, 3, 8)),
            dma((2, 2, 8)),
            dma((2, 3, 7)),
            dma((2,)),
            dma((2, 6)),
            dma((2, 4)),
            dma((2, 2, 4)),
            dma((2, 2, 3)),
            dma((2, 3)),
            dma((2, 3)),
            dma((2, 2, 4)),
            dma((2, 8)),
        ],
        compiler_params=pltpu.CompilerParams(
            collective_id=0, has_side_effects=True, vmem_limit_bytes=48 * 2**20
        ),
    )(
        *(
            pltpu.with_memory_space_constraint(array, pltpu.HBM)
            for array in (
                hidden,
                head_weight.reshape(per_section * rows, width),
                panel_section.reshape(1, -1),
                targets.reshape(1, -1),
            )
        )
    )
    loss, hidden_grad, grads = pl.pallas_call(
        write_out,
        name="write_out",
        out_shape=(
            jax.ShapeDtypeStruct((1, ROWS), f32),
            jax.ShapeDtypeStruct((2, D), f32),
            jax.ShapeDtypeStruct((NS * ROWS, D), bf16),
        ),
        in_specs=[vmem] * 3,
        out_specs=(hbm, hbm, hbm),
        scratch_shapes=[dma((2 + PIECES,))],
        compiler_params=pltpu.CompilerParams(vmem_limit_bytes=2 * 2**20),
    )(
        *(
            pltpu.with_memory_space_constraint(array, pltpu.VMEM)
            for array in (loss, hidden_grad, grads)
        )
    )
    return (loss.reshape(ROWS), hidden_grad, grads.reshape(1, NS, 2, rows, width))


def solution(mesh):
    in_specs = (P("section", None), P("section", "tensor", None), P(), P())
    out_specs = (
        P("section"),
        P(("section", "tensor"), None),
        P("section", None, None, "tensor", None),
    )
    return jax.shard_map(
        on_device, mesh=mesh, in_specs=in_specs, out_specs=out_specs, check_vma=False
    )
```
